128 devices in a mesh: blk: 64 (over z, x_hi, y, core), feat: 2 (over x_lo).
Axes of the slice: x: 4 (x_hi: 2, x_lo: 2; x = x_hi * 2 + x_lo), y: 4, z: 4, core: 2. Of those that a mesh axis runs over, the one named last changes fastest.
Arguments:
- embeddings: float32 [32768, 2048], P('blk', 'feat')
- partner: int32 [32768], P('blk'), may hold values from 0 to 32767, as said below
Outputs:
- loss: float32 [], replicated
- grads: float32 [32768, 2048], P('blk', 'feat')
The draws below stay inside these ranges and needn't reach their ends.
Inputs may be any that keep to these rules, and one draw needn't show every extreme that they name: `partner`: partner_i is never i and lies in a block at cycle distance at most 4 from the block of row i (blocks of 512 consecutive rows, block 63 next to block 0).
All inputs are finite; a program needn't handle non-finite values.
Results may differ from the reference program's by a relative error of at most 0.0003.
Values sent between devices are 32-bit elements; how exact they have to be, the bound alone decides.
No kernel may reach another device: no remote copies, remote signals or barrier semaphores. Data moves between devices by JAX's collectives and lax.ppermute only.
A program may use at most 128 MiB of HBM per device.

```python
import math
import jax
import jax.numpy as jnp
from jax import lax

D = 2048
ROWS = 512
REACH = 4
ROWS_ALL = 32768


def draw_embeddings(key, part):
    key = jax.random.fold_in(key, 1)
    keys = jax.random.split(key, 3)
    base = jax.random.normal(keys[0], (ROWS_ALL, D), jnp.float32)
    row_scale = jnp.exp(jax.random.uniform(keys[1], (ROWS_ALL, 1), jnp.float32, 0.0, math.log(10.0)))
    ramp = jnp.exp(math.log(3.0) * jnp.arange(D, dtype=jnp.float32)[None, :] / D)
    col_scale = jnp.exp(jax.random.uniform(keys[2], (1, D), jnp.float32, 0.0, math.log(10.0))) * ramp
    return (0.02 * base * row_scale * col_scale).astype(jnp.float32)


def draw_partner(key, part):
    key = jax.random.fold_in(key, 2)
    keys = jax.random.split(key, 3)
    index = jnp.arange(ROWS_ALL, dtype=jnp.int32)
    within = index % ROWS
    own_block = index // ROWS
    block_count = ROWS_ALL // ROWS
    offset = jax.random.randint(keys[0], (ROWS_ALL,), -REACH, REACH + 1, dtype=jnp.int32)
    other = jax.random.randint(keys[1], (ROWS_ALL,), 0, ROWS - 1, dtype=jnp.int32)
    anywhere = jax.random.randint(keys[2], (ROWS_ALL,), 0, ROWS, dtype=jnp.int32)
    target_row = jnp.where(offset == 0, (within + 1 + other) % ROWS, anywhere)
    result = (own_block + offset) % block_count * ROWS + target_row
    result = jnp.where(index == 0, ROWS_ALL - 1, jnp.where(index == ROWS_ALL - 1, 0, result))
    return result.astype(jnp.int32)


def setup_inputs(seed: int = 0) -> dict:
    key_of = jax.random.split(jax.random.key(seed), 3)
    embeddings = draw_embeddings(jax.random.fold_in(key_of[2], 71), 0)
    partner = draw_partner(jax.random.fold_in(key_of[2], 71), 0)
    return dict(embeddings=embeddings, partner=partner)


sharpness_divisor = 0.1
score_shift = 10.0

def band_ids(block, within):
    block_count = ROWS_ALL // ROWS
    offsets = jnp.arange(-REACH, REACH + 1, dtype=jnp.int32)
    col_blocks = (block + offsets) % block_count
    return (col_blocks[:, None] * ROWS + within[None, :]).reshape(-1).astype(jnp.int32)

def block_scores(unit, block):
    within = jnp.arange(ROWS, dtype=jnp.int32)
    row_ids = (block * ROWS + within).astype(jnp.int32)
    col_ids = band_ids(block, within)
    left_unit_embeddings = lax.dynamic_slice_in_dim(unit, block * ROWS, ROWS, 0)
    right_unit_embeddings = unit[col_ids]
    similarity_energies = jnp.dot(left_unit_embeddings, right_unit_embeddings.T, precision=lax.Precision.HIGHEST, preferred_element_type=jnp.float32) / sharpness_divisor
    kept = col_ids[None, :] != row_ids[:, None]
    return (similarity_energies, kept, row_ids, col_ids, left_unit_embeddings, right_unit_embeddings)

def reference(embeddings, partner):
    norms = jnp.sqrt(lax.optimization_barrier(jnp.sum(embeddings * embeddings, axis=1)) + 1e-06)
    unit = embeddings / norms[:, None]
    block_list = jnp.arange(ROWS_ALL // ROWS, dtype=jnp.int32)

    def first_pass(block):
        similarity_energies, kept, row_ids, col_ids, left_unit_embeddings, right_unit_embeddings = block_scores(unit, block)
        expo = jnp.where(kept, jnp.exp(similarity_energies - score_shift), 0.0)
        lse = score_shift + jnp.log(lax.optimization_barrier(jnp.sum(expo, axis=1)))
        part_rows = partner[row_ids]
        spos = lax.optimization_barrier(jnp.sum(jnp.where(col_ids[None, :] == part_rows[:, None], similarity_energies, 0.0), axis=1))
        return (lse, spos)
    lse, spos = lax.map(first_pass, block_list)
    lse = lse.reshape(-1)
    spos = spos.reshape(-1)
    counts = 1.0 + jax.ops.segment_sum(jnp.ones((ROWS_ALL,), jnp.float32), partner, num_segments=ROWS_ALL)
    loss = jnp.sum(counts * lse * 0.5 - spos) / ROWS_ALL

    def second_pass(block):
        similarity_energies, kept, row_ids, col_ids, left_unit_embeddings, right_unit_embeddings = block_scores(unit, block)
        lse_rows = lse[row_ids]
        lse_cols = lse[col_ids]
        probs = jnp.where(kept, jnp.exp(similarity_energies - lse_rows[:, None]), 0.0)
        probs_back = jnp.where(kept, jnp.exp(similarity_energies - lse_cols[None, :]), 0.0)
        hits = (col_ids[None, :] == partner[row_ids][:, None]).astype(jnp.float32)
        hits_back = (partner[col_ids][None, :] == row_ids[:, None]).astype(jnp.float32)
        mixing_coefficient_matrix = (counts[row_ids][:, None] * probs + counts[col_ids][None, :] * probs_back) * 0.5 - hits - hits_back
        derivative_wrt_unit_embeddings = jnp.dot(mixing_coefficient_matrix, right_unit_embeddings, precision=lax.Precision.HIGHEST, preferred_element_type=jnp.float32) / sharpness_divisor
        proj = lax.optimization_barrier(jnp.sum(left_unit_embeddings * derivative_wrt_unit_embeddings, axis=1))
        norm_rows = lax.dynamic_slice_in_dim(norms, block * ROWS, ROWS, 0)
        return (derivative_wrt_unit_embeddings - left_unit_embeddings * proj[:, None]) / norm_rows[:, None]
    grads = lax.map(second_pass, block_list).reshape(ROWS_ALL, D)
    return (loss, grads)
```

```python
import functools

import jax
import jax.numpy as jnp
from jax import lax
from jax.experimental import pallas as pl
from jax.experimental.pallas import tpu as pltpu
from jax.sharding import PartitionSpec as P

R = 512
F = 1024
F32 = jnp.float32
BF16 = jnp.bfloat16
VMEM = 56 * 1024 * 1024
NT = (((1,), (1,)), ((), ()))
NN = (((1,), (0,)), ((), ()))
M, E, O, X, N = range(5)
LEFT = ((M, E, O, X, O), (M, X, O, X, O))
RIGHT = ((N, N, N, N, O), (N, N, N, O, O))


def split(v):
    hi = v.astype(BF16)
    return hi, (v - hi.astype(F32)).astype(BF16)


def dot3(ah, al, bh, bl, dims):
    def one(a, b):
        return lax.dot_general(a, b, dims, preferred_element_type=F32)

    return one(ah, bh) + one(ah, bl) + one(al, bh)


def pick(par, table, s):
    even = jnp.int32(table[0][0])
    odd = jnp.int32(table[1][0])
    for k in range(1, len(table[0])):
        even = jnp.where(s == k, table[0][k], even)
        odd = jnp.where(s == k, table[1][k], odd)
    return jnp.where(par == 0, even, odd)


def scores_kernel(lefts, par_ref, *refs):
    names = sorted(set(lefts[0]) | set(lefts[1]))
    ins = dict(zip(names, refs[: len(names)]))
    right, out = refs[len(names)], refs[len(names) + 1]
    lbuf, rbuf, rh, rl, ob, lsem, rsem, osem = refs[len(names) + 2 :]
    par = par_ref[0]
    pltpu.make_async_copy(right, rbuf, rsem).start()
    for p in (0, 1):

        @pl.when(par == p)
        def _():
            for s, name in enumerate(lefts[p]):
                pltpu.make_async_copy(ins[name], lbuf.at[s], lsem.at[s]).start()

    pltpu.make_async_copy(right, rbuf, rsem).wait()
    hi, lo = split(rbuf[...])
    rh[...] = hi
    rl[...] = lo
    count = jnp.where(par == 0, len(lefts[0]), len(lefts[1]))

    def step(s, _):
        pltpu.make_async_copy(right, lbuf.at[s], lsem.at[s]).wait()

        def rows(k, _):
            at = pl.ds(pl.multiple_of(k * 128, 128), 128)
            lh, ll = split(lbuf[s, at, :])
            ob[s, at, :] = dot3(lh, ll, rh[...], rl[...], NT)
            return 0

        lax.fori_loop(0, R // 128, rows, 0)
        pltpu.make_async_copy(ob.at[s], out.at[s], osem.at[s]).start()
        return 0

    lax.fori_loop(0, count, step, 0)

    def drain(s, _):
        pltpu.make_async_copy(ob.at[s], out.at[s], osem.at[s]).wait()
        return 0

    lax.fori_loop(0, count, drain, 0)


def partial_scores(par, blocks, right, lefts):
    slots = max(len(lefts[0]), len(lefts[1]))
    names = sorted(set(lefts[0]) | set(lefts[1]))
    return pl.pallas_call(
        functools.partial(scores_kernel, lefts),
        out_shape=jax.ShapeDtypeStruct((slots, R, R), F32),
        in_specs=[pl.BlockSpec(memory_space=pltpu.SMEM)] + [pl.BlockSpec(memory_space=pl.ANY)] * (len(names) + 1),
        out_specs=pl.BlockSpec(memory_space=pl.ANY),
        scratch_shapes=[
            pltpu.VMEM((slots, R, F), F32),
            pltpu.VMEM((R, F), F32),
            pltpu.VMEM((R, F), BF16),
            pltpu.VMEM((R, F), BF16),
            pltpu.VMEM((slots, R, R), F32),
            pltpu.SemaphoreType.DMA((slots,)),
            pltpu.SemaphoreType.DMA,
            pltpu.SemaphoreType.DMA((slots,)),
        ],
        compiler_params=pltpu.CompilerParams(vmem_limit_bytes=VMEM),
        cost_estimate=pl.CostEstimate(flops=slots * 6 * R * R * F, bytes_accessed=(slots + 1) * R * F * 4, transcendentals=0),
        name="partial_scores",
    )(par, *[blocks[k] for k in names], right)


def columns(rows):
    return jnp.transpose(rows)


def sums_kernel(par_ref, mine, theirs, vec, s_out, t_out):
    s = pl.program_id(0)
    par = par_ref[0]
    left, right = pick(par, LEFT, s), pick(par, RIGHT, s)

    @pl.when(s == 0)
    def _():
        t_out[...] = jnp.zeros_like(t_out)

    inv_j = vec[right, 0:1, :]
    inv_i = columns(vec[left])[:, 0:1] * 10.0
    diag = s == 4
    for k in range(R // 128):
        at = slice(k * 128, (k + 1) * 128)
        sc = (mine[0, at, :] + theirs[0, at, :]) * (inv_i[at] * inv_j)
        s_out[0, at, :] = sc
        ex = jnp.exp(sc - 10.0)
        r = lax.broadcasted_iota(jnp.int32, (128, R), 0) + k * 128
        c = lax.broadcasted_iota(jnp.int32, (128, R), 1)
        ex = jnp.where(jnp.logical_and(diag, r == c), 0.0, ex)
        lanes = ex[:, 0:128] + ex[:, 128:256] + ex[:, 256:384] + ex[:, 384:512]
        t_out[left, 0:1, at] += jnp.sum(jnp.transpose(lanes), axis=0, keepdims=True)
        down = jnp.sum(ex, axis=0, keepdims=True)
        t_out[right, 0:1, :] += jnp.where(diag, 0.0, down)


def score_sums(par, mine, theirs, vec):
    one = lambda s: (s, 0, 0)
    whole = lambda s: (0, 0, 0)
    return pl.pallas_call(
        sums_kernel,
        grid=(5,),
        out_shape=(jax.ShapeDtypeStruct((5, R, R), F32), jax.ShapeDtypeStruct((5, 8, R), F32)),
        in_specs=[
            pl.BlockSpec(memory_space=pltpu.SMEM),
            pl.BlockSpec((1, R, R), one),
            pl.BlockSpec((1, R, R), one),
            pl.BlockSpec((5, 8, R), whole),
        ],
        out_specs=(pl.BlockSpec((1, R, R), one), pl.BlockSpec((5, 8, R), whole)),
        compiler_params=pltpu.CompilerParams(vmem_limit_bytes=VMEM),
        name="score_sums",
    )(par, mine, theirs, vec)


def coef_kernel(par_ref, sc_ref, vec, ids, ch, cl, th, tl, t_out, spos_out):
    s = pl.program_id(0)
    par = par_ref[0]
    left, right = pick(par, LEFT, s), pick(par, RIGHT, s)

    @pl.when(s == 0)
    def _():
        t_out[...] = jnp.zeros_like(t_out)
        spos_out[...] = jnp.zeros_like(spos_out)

    cols = columns(vec[left])
    part_i = cols[:, 1:2].astype(jnp.int32) - ids[right]
    a_i = cols[:, 2:3]
    part_j = vec[right, 1:2, :].astype(jnp.int32) - ids[left]
    a_j = vec[right, 2:3, :]
    diag = s == 4
    for k in range(R // 128):
        at = slice(k * 128, (k + 1) * 128)
        sc = sc_ref[0, at, :]
        r = lax.broadcasted_iota(jnp.int32, (128, R), 0) + k * 128
        c = lax.broadcasted_iota(jnp.int32, (128, R), 1)
        ex = jnp.where(jnp.logical_and(diag, r == c), 0.0, jnp.exp(sc - 10.0))
        hits = (part_i[at] == c).astype(F32)
        back = (part_j == r).astype(F32)
        cf = ex * (a_i[at] + a_j) - hits - back
        hs = sc * (hits + jnp.where(diag, 0.0, back))
        spos_out[...] += jnp.sum(hs.reshape(16, 8, R), axis=0)
        pr = cf * sc
        lanes = pr[:, 0:128] + pr[:, 128:256] + pr[:, 256:384] + pr[:, 384:512]
        t_out[left, 0:1, at] += jnp.sum(jnp.transpose(lanes), axis=0, keepdims=True)
        down = jnp.sum(pr, axis=0, keepdims=True)
        t_out[right, 0:1, :] += jnp.where(diag, 0.0, down)
        hi, lo = split(cf)
        ch[0, at, :] = hi
        cl[0, at, :] = lo
        hi, lo = split(jnp.transpose(cf))
        th[0, :, at] = hi
        tl[0, :, at] = lo


def coefficients(par, scores, vec, ids):
    one = lambda s: (s, 0, 0)
    whole = lambda s: (0, 0, 0)
    mat = pl.BlockSpec((1, R, R), one)
    half = jax.ShapeDtypeStruct((5, R, R), BF16)
    return pl.pallas_call(
        coef_kernel,
        grid=(5,),
        out_shape=(half, half, half, half, jax.ShapeDtypeStruct((5, 8, R), F32), jax.ShapeDtypeStruct((8, R), F32)),
        in_specs=[
            pl.BlockSpec(memory_space=pltpu.SMEM),
            mat,
            pl.BlockSpec((5, 8, R), whole),
            pl.BlockSpec(memory_space=pltpu.SMEM),
        ],
        out_specs=(mat, mat, mat, mat, pl.BlockSpec((5, 8, R), whole), pl.BlockSpec((8, R), lambda s: (0, 0))),
        compiler_params=pltpu.CompilerParams(vmem_limit_bytes=VMEM),
        name="coefficients",
    )(par, scores, vec, ids)


def units_kernel(m, e, o, x, n, vec, uh, ul):
    k = pl.program_id(0)
    for j, ref in enumerate((m, e, o, x, n)):
        inv = columns(vec[j])[:, 0:1]
        hi, lo = split(ref[...] * inv)
        uh[j] = hi
        ul[j] = lo


def split_units(blocks, vec):
    cell = pl.BlockSpec((R, 256), lambda k: (0, k))
    res = pl.BlockSpec((5, R, 256), lambda k: (0, 0, k))
    shape = jax.ShapeDtypeStruct((5, R, F), BF16)
    return pl.pallas_call(
        units_kernel,
        grid=(F // 256,),
        out_shape=(shape, shape),
        in_specs=[cell] * 5 + [pl.BlockSpec((5, 8, R), lambda k: (0, 0, 0))],
        out_specs=(res, res),
        compiler_params=pltpu.CompilerParams(vmem_limit_bytes=VMEM),
        name="split_units",
    )(*blocks, vec)


def contrib_kernel(plans, par_ref, ch, cl, th, tl, uh, ul, proj, *refs):
    outs = refs
    par = par_ref[0]
    f = pl.program_id(0)
    for p in (0, 1):

        @pl.when(par == p)
        def _():
            for (name, terms), out in zip(plans[p], outs):
                total = None
                for transposed, s, u in terms:
                    a = (th, tl) if transposed else (ch, cl)
                    t = dot3(a[0][s], a[1][s], uh[u], ul[u], NN)
                    total = t if total is None else total + t
                if total is not None:
                    out[0:R, :] = total
                else:
                    out[0:R, :] = jnp.zeros((R, out.shape[1]), F32)
                out[R : R + 8, 0:R] = proj[name]


def contributions(par, mats, units, proj, plans):
    T = 512
    whole = pl.BlockSpec((5, R, R), lambda f: (0, 0, 0))
    cell = pl.BlockSpec((5, R, T), lambda f: (0, 0, f))
    count = len(plans[0])
    terms = sum(len(t) for _, t in plans[0])
    return pl.pallas_call(
        functools.partial(contrib_kernel, plans),
        grid=(F // T,),
        out_shape=[jax.ShapeDtypeStruct((R + 8, F), F32)] * count,
        in_specs=[pl.BlockSpec(memory_space=pltpu.SMEM)] + [whole] * 4 + [cell] * 2 + [pl.BlockSpec((5, 8, R), lambda f: (0, 0, 0))],
        out_specs=[pl.BlockSpec((R + 8, T), lambda f: (0, f))] * count,
        compiler_params=pltpu.CompilerParams(vmem_limit_bytes=VMEM),
        cost_estimate=pl.CostEstimate(flops=terms * 6 * R * R * F, bytes_accessed=terms * R * F * 8, transcendentals=0),
        name="contributions",
    )(par, *mats, *units, proj)


PLAN_OUT = (
    ((N, ((1, 0, M), (1, 1, E), (1, 2, O), (1, 3, X))), (E, ((0, 1, N),)), (M, ((0, 0, N),))),
    ((N, ((1, 0, M), (1, 1, X), (1, 2, O))), (E, ()), (M, ((0, 0, N),))),
)
PLAN_IN = (
    ((X, ((0, 3, N),)), (O, ((0, 2, N), (0, 4, O)))),
    ((X, ((0, 1, N), (0, 3, O))), (O, ((0, 2, N), (1, 3, X), (0, 4, O)))),
)


def per_device(embeddings, partner):
    blk = lax.axis_index("blk")
    count = lax.axis_size("blk")
    par1 = (blk % 2).astype(jnp.int32)
    par = par1.reshape(1)
    even = par1 == 0

    def shift(v, steps):
        return lax.ppermute(v, "blk", [(i, (i + steps) % count) for i in range(count)])

    def cores(v):
        return lax.ppermute(v, "blk", [(i, i ^ 1) for i in range(count)])

    def feats(v):
        return lax.ppermute(v, "feat", [(0, 1), (1, 0)])

    own = embeddings
    right = shift(own, -2)
    left = shift(own, 2)
    other = cores(own)

    ss = jnp.sum(own * own, axis=1)
    inv = 1.0 / jnp.sqrt(ss + feats(ss) + 1e-06)
    pack = jnp.stack([inv, partner.astype(F32)])
    pack_x = cores(pack)
    node = jnp.where(even, jnp.stack([pack, pack_x]), jnp.stack([pack_x, pack]))
    node_l, node_r = shift(node, 2), shift(node, -2)
    far_l, far_r = shift(node[:, 1], 4), shift(node[:, 1], -4)
    near = jnp.concatenate([far_l, node_l[:, 1], node[:, 1], node_r[:, 1], far_r], axis=0).reshape(-1, 1)
    row_ids = blk * R + jnp.arange(R, dtype=jnp.int32)
    counts = 1.0 + jnp.sum((near == row_ids.astype(F32)[None, :]).astype(F32), axis=0)

    def vectors(cells):
        v = jnp.stack(cells)
        return jnp.pad(v, ((0, 0), (0, 8 - v.shape[1]), (0, 0)))

    mine = lambda v: jnp.where(even, v[0], v[1])
    packs = [mine(node_l), node_l[1], pack, pack_x, mine(node_r)]
    vec = vectors(packs)
    ids = (
        jnp.stack([blk + count - 2, blk + count - 1, blk, blk + 1 - 2 * par1, blk + 2]) % count * R
    ).astype(jnp.int32)

    near_scores = partial_scores(par, {O: own, X: other}, own, ((O,), (O, X)))
    extra = lax.ppermute(left, "blk", [(i + 1, i) for i in range(0, count, 2)])
    far_scores = partial_scores(
        par, {M: left, E: extra, O: own, X: other}, right, ((M, E, O, X), (M, X, O))
    )
    near_got = feats(near_scores)
    far_got = feats(far_scores)

    def slots(near, far):
        return jnp.concatenate([far[0:3], jnp.where(even, far[3:4], near[1:2]), near[0:1]], axis=0)

    units = split_units([left, extra, own, other, right], vec)
    scores, sums = score_sums(par, slots(near_scores, far_scores), slots(near_got, far_got), vec)
    sums = sums[:, 0]

    def home(v):
        to_prev = [(i, (i - 1) % count) for i in range(0, count, 2)]
        return v[O] + cores(v[X]) + shift(v[N], 2) + shift(v[M], -2) + lax.ppermute(v[E], "blk", to_prev)

    total = home(sums)
    lse = 10.0 + jnp.log(total)
    a = counts * 0.5 / total
    from_prev = [((i - 1) % count, i) for i in range(0, count, 2)]
    a_all = [shift(a, 2), lax.ppermute(a, "blk", from_prev), a, cores(a), shift(a, -2)]
    vec2 = vectors([jnp.concatenate([p, q[None]], axis=0) for p, q in zip(packs, a_all)])

    ch, cl, th, tl, proj, spos = coefficients(par, scores, vec2, ids)
    mats = (ch, cl, th, tl)
    to_right, to_prev, to_left = contributions(par, mats, units, proj, PLAN_OUT)
    got_next = lax.ppermute(to_prev, "blk", [(i, (i - 1) % count) for i in range(0, count, 2)])
    to_other, kept = contributions(par, mats, units, proj, PLAN_IN)
    from_left = shift(to_right, 2)
    from_right = shift(to_left, -2)
    from_other = cores(to_other)

    loss = jnp.sum(counts * lse) * 0.5 - jnp.sum(spos)
    step = 1
    while step < count:
        loss = loss + lax.ppermute(loss, "blk", [(i, i ^ step) for i in range(count)])
        step *= 2
    loss = loss / (count * R)

    grad = kept + from_left + from_right + from_other + got_next
    along = grad[R, 0:R]
    grads = (grad[0:R] * 10.0 - own * (inv * along)[:, None]) * inv[:, None]
    return (loss, grads)


def solution(mesh):
    in_specs = (P("blk", "feat"), P("blk"))
    out_specs = (P(), P("blk", "feat"))
    return jax.shard_map(per_device, mesh=mesh, in_specs=in_specs, out_specs=out_specs, check_vma=False)
```

```python
import functools

import jax
import jax.numpy as jnp
from jax import lax
from jax.experimental import pallas as pl
from jax.experimental.pallas import tpu as pltpu
from jax.sharding import PartitionSpec as P

R = 512
H = 256
F = 1024
F32 = jnp.float32
BF16 = jnp.bfloat16
VMEM = 56 * 1024 * 1024
NT = (((1,), (1,)), ((), ()))
NN = (((1,), (0,)), ((), ()))
TN = (((0,), (0,)), ((), ()))
M, E, O, X, N = range(5)
LEFT = ((O, X, M, E, O), (O, X, M, X, O))
RIGHT = ((N, N, N, N, O), (N, N, N, O, O))
SMEM_SPEC = pl.BlockSpec(memory_space=pltpu.SMEM)
ANY_SPEC = pl.BlockSpec(memory_space=pl.ANY)
FULL = pl.BlockSpec(memory_space=pltpu.VMEM)
PARAMS = pltpu.CompilerParams(vmem_limit_bytes=VMEM)


def split(v):
    hi = v.astype(BF16)
    return hi, (v - hi.astype(F32)).astype(BF16)


def dot3(ah, al, bh, bl, dims):
    def one(a, b):
        return lax.dot_general(a, b, dims, preferred_element_type=F32)

    return one(ah, bh) + one(ah, bl) + one(al, bh)


def pick(par, table, s):
    if isinstance(s, int):
        return jnp.where(par == 0, table[0][s], table[1][s])
    even = jnp.int32(table[0][0])
    odd = jnp.int32(table[1][0])
    for k in range(1, len(table[0])):
        even = jnp.where(s == k, table[0][k], even)
        odd = jnp.where(s == k, table[1][k], odd)
    return jnp.where(par == 0, even, odd)


def fold(v):
    lanes = v[:, 0:128]
    for k in range(1, v.shape[1] // 128):
        lanes = lanes + v[:, k * 128 : (k + 1) * 128]
    return jnp.sum(jnp.transpose(lanes), axis=0, keepdims=True)


def scores_kernel(nsq, first, only, meta, l0, l1, right, *refs):
    if only is None:
        out_a, kh, kl = refs[:3]
        out_b = None
        scratch = refs[3:]
    else:
        out_a, out_b, kh, kl = refs[:4]
        scratch = refs[4:]
    buf, hb, lb, ob, sq, isem, hsem, osem = scratch
    par = meta[0]
    sources = {0: right, 2: l1} if first else {0: right, 1: l0, 2: l1}
    ins = {k: pltpu.make_async_copy(src.at[0:R], buf.at[k], isem.at[k]) for k, src in sources.items()}
    for copy in ins.values():
        copy.start()
    sq[...] = jnp.zeros_like(sq)
    kept = {"near": (0, 2), "a": (0,), "b": (1, 2)}[nsq]

    def hold(k):
        if k in kept:
            j = kept.index(k)
            for t, (src, dst) in enumerate(((hb, kh), (lb, kl))):
                yield pltpu.make_async_copy(src.at[k], dst.at[j], hsem.at[j, t])

    def ready(k):
        ins[k].wait()
        for q in range(4):
            at = slice(q * 128, (q + 1) * 128)
            v = buf[k, at, :]
            hi, lo = split(v)
            hb[k, at, :] = hi
            lb[k, at, :] = lo
            if k in kept:
                sq[kept.index(k) : kept.index(k) + 1, at] = fold(v * v)
        for c in hold(k):
            c.start()

    def score(slot, k):
        ob[slot * R : (slot + 1) * R, :] = dot3(hb[k], lb[k], hb[0], lb[0], NT)

    ready(0)
    if not first:
        ready(1)
    score(0, 0 if first else 1)
    ready(2)
    if only is None:
        score(1, 2)
        outs = [pltpu.make_async_copy(ob, out_a.at[0 : 2 * R], osem.at[0])]
    else:
        outs = [pltpu.make_async_copy(ob.at[0:R], out_a.at[0:R], osem.at[0])]
    rows = out_a.shape[0] - 8
    outs.append(pltpu.make_async_copy(sq, out_a.at[rows : rows + 8], osem.at[1]))
    for c in outs:
        c.start()
    if only is not None:

        @pl.when(par == only)
        def _():
            score(1, 2)
            last = pltpu.make_async_copy(ob.at[R : 2 * R], out_b, osem.at[2])
            last.start()
            last.wait()

    for k in kept:
        for c in hold(k):
            c.wait()
    for c in outs:
        c.wait()


def partial_scores(meta, l0, l1, right, nsq, first, only):
    nkeep = {"near": 2, "a": 1, "b": 2}[nsq]
    slots = 2 if only is None else 1
    half = jax.ShapeDtypeStruct((nkeep, R, F), BF16)
    shapes = [jax.ShapeDtypeStruct((slots * R + 8, R), F32)]
    if only is not None:
        shapes.append(jax.ShapeDtypeStruct((R, R), F32))
    shapes += [half, half]
    return pl.pallas_call(
        functools.partial(scores_kernel, nsq, first, only),
        out_shape=shapes,
        in_specs=[SMEM_SPEC] + [ANY_SPEC] * 3,
        out_specs=[ANY_SPEC] * len(shapes),
        scratch_shapes=[
            pltpu.VMEM((3, R, F), F32),
            pltpu.VMEM((3, R, F), BF16),
            pltpu.VMEM((3, R, F), BF16),
            pltpu.VMEM((2 * R, R), F32),
            pltpu.VMEM((8, R), F32),
            pltpu.SemaphoreType.DMA((3,)),
            pltpu.SemaphoreType.DMA((2, 2)),
            pltpu.SemaphoreType.DMA((3,)),
        ],
        compiler_params=PARAMS,
        cost_estimate=pl.CostEstimate(flops=12 * R * R * F, bytes_accessed=8 * R * F * 4, transcendentals=0),
        name="partial_scores",
    )(meta, l0, l1, right)


def sums_kernel(ids, only, meta, *refs):
    if only is None:
        mine, theirs, vec, s_out, t_out, p_out = refs
        mine_b = theirs_b = s_out_b = None
    else:
        mine, theirs, mine_b, theirs_b, vec, s_out, s_out_b, t_out, p_out = refs
    g = pl.program_id(0)
    par = meta[0]
    part = g % 2

    @pl.when(g == 0)
    def _():
        t_out[...] = jnp.zeros_like(t_out)
        p_out[...] = jnp.zeros_like(p_out)

    def half(slot, a, b, out):
        left, right = pick(par, LEFT, slot), pick(par, RIGHT, slot)
        base_l, base_r = meta[1 + left], meta[1 + right]
        diag = slot == 4
        cols = jnp.transpose(vec[left])
        pick_rows = lambda v: jnp.where(part == 0, v[0:H], v[H:R])
        inv_i = pick_rows(cols[:, 0:1]) * 10.0
        part_i = pick_rows(cols[:, 1:2]).astype(jnp.int32) - base_r
        inv_j = vec[right, 0:1, :]
        part_j = vec[right, 1:2, :].astype(jnp.int32) - base_l
        down = jnp.zeros((8, R), F32)
        down_n = jnp.zeros((8, R), F32)
        spos = jnp.zeros((8, R), F32)
        for k in range(H // 128):
            at = slice(k * 128, (k + 1) * 128)
            sc = (a[at, :] + b[at, :]) * (inv_i[at] * inv_j)
            out[at, :] = sc
            r = lax.broadcasted_iota(jnp.int32, (128, R), 0) + (k * 128 + part * H)
            c = lax.broadcasted_iota(jnp.int32, (128, R), 1)
            ex = jnp.exp(sc - 10.0)
            if diag:
                ex = jnp.where(r == c, 0.0, ex)
            hits = part_i[at] == c
            back = part_j == r
            pos = jnp.where(hits, sc, 0.0)
            if not diag:
                pos += jnp.where(back, sc, 0.0)
            spos += jnp.sum(pos.reshape(16, 8, R), axis=0)
            here = pl.ds(pl.multiple_of(part * H + k * 128, 128), 128)
            t_out[left, 0:1, here] += fold(ex)
            t_out[left, 1:2, here] += fold(jnp.where(back, 1.0, 0.0))
            if not diag:
                down += jnp.sum(ex.reshape(16, 8, R), axis=0)
                down_n += jnp.sum(jnp.where(hits, 1.0, 0.0).reshape(16, 8, R), axis=0)
        if not diag:
            t_out[right, 0:1, :] += jnp.sum(down, axis=0, keepdims=True)
            t_out[right, 1:2, :] += jnp.sum(down_n, axis=0, keepdims=True)
        p_out[...] += spos

    pl.when(g < 2)(lambda: half(ids[0], mine, theirs, s_out))
    if only is None:
        pl.when(g >= 2)(lambda: half(ids[1], mine, theirs, s_out))
    else:
        pl.when(jnp.logical_and(g >= 2, par == only))(lambda: half(ids[1], mine_b, theirs_b, s_out_b))


def score_sums(meta, mine, theirs, vec, ids, only):
    tail = (jax.ShapeDtypeStruct((5, 8, R), F32), jax.ShapeDtypeStruct((8, R), F32))
    tail_specs = (pl.BlockSpec((5, 8, R), lambda g: (0, 0, 0)), pl.BlockSpec((8, R), lambda g: (0, 0)))
    vec_spec = pl.BlockSpec((5, 8, R), lambda g: (0, 0, 0))
    mat = jax.ShapeDtypeStruct((R, R), F32)
    if only is None:
        cell = pl.BlockSpec((H, R), lambda g: (g, 0))
        ops, specs = (mine[0], theirs[0]), [cell, cell]
        shapes, outs = (jax.ShapeDtypeStruct((2 * R, R), F32),), (cell,)
    else:
        a = pl.BlockSpec((H, R), lambda g: (jnp.minimum(g, 1), 0))
        b = pl.BlockSpec((H, R), lambda g: (jnp.maximum(g - 2, 0), 0))
        ops, specs = (mine[0], theirs[0], mine[1], theirs[1]), [a, a, b, b]
        shapes, outs = (mat, mat), (a, b)
    return pl.pallas_call(
        functools.partial(sums_kernel, ids, only),
        grid=(4,),
        out_shape=shapes + tail,
        in_specs=[SMEM_SPEC] + specs + [vec_spec],
        out_specs=outs + tail_specs,
        compiler_params=PARAMS,
        cost_estimate=pl.CostEstimate(flops=12 * R * R * F, bytes_accessed=8 * R * F * 4, transcendentals=0),
        name="score_sums",
    )(meta, *ops, vec)


def coef_kernel(meta, s01, s2, s3e, s3o, s4, vec, nh, nl, oh, ol, rh, rl, ch, cl, m_out, y_out, t_out,
                sbuf, rbh, rbl, cbh, cbl, uh, ul, ssem, usem, csem):
    par = meta[0]

    def load(s, src):
        pltpu.make_async_copy(src, sbuf.at[s], ssem.at[s]).start()

    load(2, s2)
    pl.when(par == 0)(lambda: load(3, s3e))
    pl.when(par == 1)(lambda: load(3, s3o))
    load(0, s01.at[0:R])
    load(1, s01.at[R : 2 * R])
    load(4, s4)
    units = [
        pltpu.make_async_copy(src, dst, usem.at[k])
        for k, (src, dst) in enumerate(((nh.at[0], uh.at[0]), (nl.at[0], ul.at[0]), (oh.at[0], uh.at[1]), (ol.at[0], ul.at[1])))
    ]
    for u in units:
        u.start()
    t_out[...] = jnp.zeros_like(t_out)

    def out_copies(s):
        out = [
            pltpu.make_async_copy(rbh.at[s], rh.at[s], csem.at[s, 0]),
            pltpu.make_async_copy(rbl.at[s], rl.at[s], csem.at[s, 1]),
        ]
        if s < 4:
            out += [
                pltpu.make_async_copy(cbh.at[s], ch.at[s], csem.at[s, 2]),
                pltpu.make_async_copy(cbl.at[s], cl.at[s], csem.at[s, 3]),
            ]
        return out

    def slot(s):
        pltpu.make_async_copy(s2, sbuf.at[s], ssem.at[s]).wait()
        left, right = pick(par, LEFT, s), pick(par, RIGHT, s)
        cols = jnp.transpose(vec[left])
        inv_i = cols[:, 0:1]
        part_i = cols[:, 1:2].astype(jnp.int32) - meta[1 + right]
        a_i = cols[:, 2:3]
        inv_j = vec[right, 0:1, :]
        part_j = vec[right, 1:2, :].astype(jnp.int32) - meta[1 + left]
        a_j = vec[right, 2:3, :]
        diag = s == 4
        down = jnp.zeros((8, R), F32)
        for k in range(R // 128):
            at = slice(k * 128, (k + 1) * 128)
            sc = sbuf[s, at, :]
            r = lax.broadcasted_iota(jnp.int32, (128, R), 0) + k * 128
            c = lax.broadcasted_iota(jnp.int32, (128, R), 1)
            ex = jnp.exp(sc - 10.0)
            if diag:
                ex = jnp.where(r == c, 0.0, ex)
            cf = ex * (a_i[at] + a_j)
            cf = jnp.where(part_i[at] == c, cf - 1.0, cf)
            cf = jnp.where(part_j == r, cf - 1.0, cf)
            pr = cf * sc
            t_out[left, 0:1, at] += fold(pr)
            hi, lo = split(cf * inv_j)
            rbh[s, at, :] = hi
            rbl[s, at, :] = lo
            if not diag:
                down += jnp.sum(pr.reshape(16, 8, R), axis=0)
                hi, lo = split(cf * inv_i[at])
                cbh[s, at, :] = hi
                cbl[s, at, :] = lo
        if not diag:
            t_out[right, 0:1, :] += jnp.sum(down, axis=0, keepdims=True)
        for c in out_copies(s):
            c.start()

    for s in (2, 3, 0, 1, 4):
        slot(s)
    for u in units:
        u.wait()
    m_out[0:R, :] = dot3(rbh[2], rbl[2], uh[0], ul[0], NN)
    m_out[R : R + 8, 0:R] = t_out[M]
    y_out[0:R, :] = dot3(rbh[3], rbl[3], uh[par], ul[par], NN)
    y_out[R : R + 8, 0:R] = t_out[E]
    for s in range(5):
        for c in out_copies(s):
            c.wait()


def coefficients(meta, scores, vec, n_halves, o_halves):
    half = lambda n: jax.ShapeDtypeStruct((n, R, R), BF16)
    part = jax.ShapeDtypeStruct((R + 8, F), F32)
    return pl.pallas_call(
        coef_kernel,
        out_shape=(half(5), half(5), half(4), half(4), part, part, jax.ShapeDtypeStruct((5, 8, R), F32)),
        in_specs=[SMEM_SPEC] + [ANY_SPEC] * 5 + [FULL] + [ANY_SPEC] * 4,
        out_specs=(ANY_SPEC,) * 4 + (FULL,) * 3,
        scratch_shapes=[
            pltpu.VMEM((5, R, R), F32),
            pltpu.VMEM((5, R, R), BF16),
            pltpu.VMEM((5, R, R), BF16),
            pltpu.VMEM((4, R, R), BF16),
            pltpu.VMEM((4, R, R), BF16),
            pltpu.VMEM((2, R, F), BF16),
            pltpu.VMEM((2, R, F), BF16),
            pltpu.SemaphoreType.DMA((5,)),
            pltpu.SemaphoreType.DMA((4,)),
            pltpu.SemaphoreType.DMA((5, 4)),
        ],
        compiler_params=PARAMS,
        cost_estimate=pl.CostEstimate(flops=12 * R * R * F, bytes_accessed=8 * R * F * 4, transcendentals=0),
        name="coefficients",
    )(meta, *scores, vec, *n_halves, *o_halves)


def right_kernel(part, meta, ch, cl, oxh, oxl, meh, mel, proj, *refs):
    if part == 1:
        out, cbh, cbl, ubh, ubl, sem = refs
    else:
        rh, rl, nh, nl, out, x_out, cbh, cbl, ubh, ubl, sem, xbh, xbl, ybh, ybl, xsem = refs
        extra = [
            pltpu.make_async_copy(src, dst, xsem.at[k])
            for k, (src, dst) in enumerate(((rh.at[1], xbh), (rl.at[1], xbl), (nh.at[0], ybh), (nl.at[0], ybl)))
        ]
    par = meta[0]
    sources = ((oxh, oxl, 0), (oxh, oxl, 1), (meh, mel, 0), (meh, mel, 1))
    at = pl.ds(part * (F // 2), F // 2)

    def copies(t):
        h, l, k = sources[t]
        return (
            pltpu.make_async_copy(ch.at[t], cbh.at[t], sem.at[t, 0]),
            pltpu.make_async_copy(cl.at[t], cbl.at[t], sem.at[t, 1]),
            pltpu.make_async_copy(h.at[k, :, at], ubh.at[t], sem.at[t, 2]),
            pltpu.make_async_copy(l.at[k, :, at], ubl.at[t], sem.at[t, 3]),
        )

    def start(t):
        for c in copies(t):
            c.start()

    def term(t):
        for c in copies(t):
            c.wait()
        part = dot3(cbh[t], cbl[t], ubh[t], ubl[t], TN)
        if t == 0:
            out[0:R, :] = part
        else:
            out[0:R, :] += part

    for t in range(3):
        start(t)
    pl.when(par == 0)(lambda: start(3))
    if part == 0:
        out[R : R + 8, 0:R] = proj[N]
        for c in extra:
            c.start()
    for t in range(3):
        term(t)
    pl.when(par == 0)(lambda: term(3))
    if part == 0:
        for c in extra:
            c.wait()
        x_out[R : R + 8, 0:R] = proj[X]
        x_out[0:R, :] = dot3(xbh[...], xbl[...], ybh[...], ybl[...], NN)


def right_part(part, meta, mats, units, proj, more=()):
    shape = jax.ShapeDtypeStruct((R + 8 * (1 - part), F // 2), F32)
    whole = jax.ShapeDtypeStruct((R + 8, F), F32)
    return pl.pallas_call(
        functools.partial(right_kernel, part),
        out_shape=shape if part else (shape, whole),
        in_specs=[SMEM_SPEC] + [ANY_SPEC] * 6 + [FULL] + [ANY_SPEC] * len(more),
        out_specs=FULL if part else (FULL, FULL),
        scratch_shapes=[
            pltpu.VMEM((4, R, R), BF16),
            pltpu.VMEM((4, R, R), BF16),
            pltpu.VMEM((4, R, F // 2), BF16),
            pltpu.VMEM((4, R, F // 2), BF16),
            pltpu.SemaphoreType.DMA((4, 4)),
        ]
        + [pltpu.VMEM((R, R), BF16)] * 2 * (1 - part)
        + [pltpu.VMEM((R, F), BF16)] * 2 * (1 - part)
        + [pltpu.SemaphoreType.DMA((4,))] * (1 - part),
        compiler_params=PARAMS,
        cost_estimate=pl.CostEstimate(flops=12 * R * R * F, bytes_accessed=8 * R * F * 4, transcendentals=0),
        name="right_part",
    )(meta, *mats, *units, proj, *more)


def own_kernel(meta, rh, rl, ch, cl, oxh, oxl, nh, nl, proj, o_out, cbh, cbl, ubh, ubl, csem, usem):
    par = meta[0]
    mats = ((rh, rl, 0), (rh, rl, 4), (ch, cl, 3))
    units = ((nh, nl, 0), (oxh, oxl, 0), (oxh, oxl, 1))

    def copies(k, source, bufs, sem):
        h, l, j = source
        return (
            pltpu.make_async_copy(h.at[j], bufs[0].at[k], sem.at[k, 0]),
            pltpu.make_async_copy(l.at[j], bufs[1].at[k], sem.at[k, 1]),
        )

    every = [copies(k, u, (ubh, ubl), usem) for k, u in enumerate(units)]
    every += [copies(k, m, (cbh, cbl), csem) for k, m in enumerate(mats)]
    for group in every:
        for c in group:
            c.start()
    for group in every:
        for c in group:
            c.wait()
    o_out[R : R + 8, 0:R] = proj[O]
    o_out[0:R, :] = dot3(cbh[0], cbl[0], ubh[0], ubl[0], NN)
    o_out[0:R, :] += dot3(cbh[1], cbl[1], ubh[1], ubl[1], NN)

    @pl.when(par == 1)
    def _():
        o_out[0:R, :] += dot3(cbh[2], cbl[2], ubh[2], ubl[2], TN)


def own_part(meta, rows, cols, ox, n, proj):
    part = jax.ShapeDtypeStruct((R + 8, F), F32)
    return pl.pallas_call(
        own_kernel,
        out_shape=part,
        in_specs=[SMEM_SPEC] + [ANY_SPEC] * 8 + [FULL],
        out_specs=FULL,
        scratch_shapes=[
            pltpu.VMEM((3, R, R), BF16),
            pltpu.VMEM((3, R, R), BF16),
            pltpu.VMEM((3, R, F), BF16),
            pltpu.VMEM((3, R, F), BF16),
            pltpu.SemaphoreType.DMA((3, 2)),
            pltpu.SemaphoreType.DMA((3, 2)),
        ],
        compiler_params=PARAMS,
        cost_estimate=pl.CostEstimate(flops=12 * R * R * F, bytes_accessed=8 * R * F * 4, transcendentals=0),
        name="own_part",
    )(meta, *rows, *cols, *ox, *n, proj)


def per_device(embeddings, partner):
    blk = lax.axis_index("blk")
    count = lax.axis_size("blk")
    par = (blk % 2).astype(jnp.int32)
    even = par == 0

    def shift(v, steps):
        return lax.ppermute(v, "blk", [(i, (i + steps) % count) for i in range(count)])

    def cores(v):
        return lax.ppermute(v, "blk", [(i, i ^ 1) for i in range(count)])

    def outwards(v):
        return lax.ppermute(v, "blk", [(i, (i + (2 if i % 2 else -2)) % count) for i in range(count)])

    def feats(v, only=None):
        if only is None:
            return lax.ppermute(v, "feat", [(0, 1), (1, 0)])
        pairs = [(2 * i + f, 2 * i + 1 - f) for i in range(only, count, 2) for f in (0, 1)]
        return lax.ppermute(v, ("blk", "feat"), pairs)

    own = embeddings
    line = jnp.pad(partner.astype(F32)[None], ((0, 7), (0, F - R)))
    block = jnp.concatenate([own, line], axis=0)
    right = shift(block, -2)
    left = shift(block, 2)
    other = cores(block)
    names = jnp.stack([blk + count - 2, blk + count - 1, blk, blk + 1 - 2 * par, blk + 2]) % count
    meta = jnp.concatenate([par[None], names.astype(jnp.int32) * R])

    def inverse(mine, theirs):
        return 1.0 / jnp.sqrt(mine + theirs + 1e-06)

    def vectors(cells):
        zero = jnp.zeros((R,), F32)
        full = [c + [zero] * (8 - len(c)) for c in cells]
        return jnp.stack([jnp.stack(c) for c in full])

    near_a, near_b, oxh, oxl = partial_scores(meta, block, other, block, "near", True, 1)
    near_ga, near_gb = feats(near_a), feats(near_b, 1)
    inv_o, inv_x = inverse(near_a[R], near_ga[R]), inverse(near_a[R + 1], near_ga[R + 1])
    who = lambda b: b[R, 0:R]
    vec_near = vectors([[], [], [inv_o, who(block)], [inv_x, who(other)], []])
    s4, s3o, near_t, near_p = score_sums(meta, (near_a, near_b), (near_ga, near_gb), vec_near, (4, 3), 1)

    extra = lax.ppermute(left, "blk", [(i + 1, i) for i in range(0, count, 2)])
    right, near_ga, near_gb = lax.optimization_barrier((right, near_ga, near_gb))
    far_a, nh, nl = partial_scores(meta, block, other, right, "a", False, None)
    far_ga = feats(far_a)
    left, extra, nh = lax.optimization_barrier((left, extra, nh))
    far_b, far_c, meh, mel = partial_scores(meta, left, extra, right, "b", False, 0)
    far_gb, far_gc = feats(far_b), feats(far_c, 0)
    inv_n = inverse(far_a[2 * R], far_ga[2 * R])
    vec_a = vectors([[], [], [inv_o, who(block)], [inv_x, who(other)], [inv_n, who(right)]])
    s01, a_t, a_p = score_sums(meta, (far_a,), (far_ga,), vec_a, (0, 1), None)
    far_gb, far_gc, a_t = lax.optimization_barrier((far_gb, far_gc, a_t))
    inv_m, inv_e = inverse(far_b[R], far_gb[R]), inverse(far_b[R + 1], far_gb[R + 1])
    packs = [[inv_m, who(left)], [inv_e, who(extra)], [inv_o, who(block)], [inv_x, who(other)], [inv_n, who(right)]]
    s2, s3e, b_t, b_p = score_sums(meta, (far_b, far_c), (far_gb, far_gc), vectors(packs), (2, 3), 0)

    t = (near_t + a_t + b_t)[:, 0:2]
    p = jnp.sum(near_p + a_p + b_p, axis=0)
    zero = jnp.zeros((2, R), F32)
    spos = jnp.stack([p, p * 0.0])
    chip = jnp.where(
        even, jnp.stack([t[M], t[E], t[O], t[X], t[N], zero, spos]), jnp.stack([zero, t[M], t[X], t[O], zero, t[N], spos])
    )
    chip = chip + cores(chip)
    got = outwards(jnp.where(even, chip[0:2], chip[4:6]))
    total = chip[2:4] + (got + cores(got))
    counts = total[:, 1] + 1.0
    a = counts * 0.5 / total[:, 0]
    a_one = outwards(a)
    a_two = cores(a_one)
    a_l, a_r = jnp.where(even, a_two, a_one), jnp.where(even, a_one, a_two)
    mine = lambda v: jnp.where(even, v[0], v[1])
    a_all = [mine(a_l), a_l[1], mine(a), mine(a[::-1]), mine(a_r)]
    vec = vectors([p + [q] for p, q in zip(packs, a_all)])

    def both(v, k):
        return v + lax.ppermute(v, "blk", [(i, i ^ k) for i in range(count)])

    loss = jnp.sum(counts * (10.0 + jnp.log(total[:, 0]))) * 0.5 - jnp.sum(chip[6, 0])
    loss, vec = lax.optimization_barrier((both(loss, 2), vec))

    rh, rl, ch, cl, to_left, swap, proj = coefficients(meta, (s01, s2, s3e, s3o, s4), vec, (nh, nl), (oxh, oxl))
    loss = both(loss, 4)
    swapped = cores(swap)
    units = (oxh, oxl, meh, mel)
    to_right, to_other = right_part(0, meta, (ch, cl), units, proj, (rh, rl, nh, nl))
    from_other = cores(to_other)
    to_right, swapped, loss = lax.optimization_barrier((to_right, swapped, loss))
    to_left = to_left + jnp.where(even, 0.0, swapped)
    ch, to_left = lax.optimization_barrier((ch, to_left))
    from_right = shift(to_left, -2)
    from_left = shift(to_right, 2)
    to_right_2 = right_part(1, meta, (ch, cl), units, proj)
    from_left_2 = shift(to_right_2, 2)
    loss, to_right_2 = lax.optimization_barrier((loss, to_right_2))
    loss = both(both(loss, 16), 32)
    loss, rh = lax.optimization_barrier((loss, rh))
    kept = own_part(meta, (rh, rl), (ch, cl), (oxh, oxl), (nh, nl), proj)
    loss, kept = lax.optimization_barrier((loss, kept))
    kept = kept + from_other + jnp.where(even, swapped, 0.0)
    loss = both(loss, 8) / (count * R)

    along = (kept + from_right)[R, 0:R] + from_left[R]
    grad = (kept + from_right)[0:R] + jnp.concatenate([from_left[0:R], from_left_2], axis=1)
    grads = (grad * 10.0 - own * (inv_o * along)[:, None]) * inv_o[:, None]
    return (loss, grads)


def solution(mesh):
    in_specs = (P("blk", "feat"), P("blk"))
    out_specs = (P(), P("blk", "feat"))
    return jax.shard_map(per_device, mesh=mesh, in_specs=in_specs, out_specs=out_specs, check_vma=False)
```

```python
import functools

import jax
import jax.numpy as jnp
from jax import lax
from jax.experimental import pallas as pl
from jax.experimental.pallas import tpu as pltpu
from jax.sharding import PartitionSpec as P

R = 512
H = 256
F = 1024
F32 = jnp.float32
BF16 = jnp.bfloat16
NT = (((1,), (1,)), ((), ()))
NN = (((1,), (0,)), ((), ()))
TN = (((0,), (0,)), ((), ()))
M, E, O, X, N = range(5)
PAR, BASE, OWN_PAIR, W_PAIR, W_NAME, W_RIGHT, EVEN, ODD, ALWAYS = 0, 1, 6, 7, 8, 9, 10, 11, 12
SMEM_SPEC = pl.BlockSpec(memory_space=pltpu.SMEM)
ANY_SPEC = pl.BlockSpec(memory_space=pl.ANY)
FULL = pl.BlockSpec(memory_space=pltpu.VMEM)
PARAMS = pltpu.CompilerParams(vmem_limit_bytes=56 * 1024 * 1024)
COST = pl.CostEstimate(flops=12 * R * R * F, bytes_accessed=8 * R * F * 4, transcendentals=0)
WHOLE = jax.ShapeDtypeStruct((R + 8, F), F32)
MAT = jax.ShapeDtypeStruct((R, R), F32)


def split(v):
    hi = v.astype(BF16)
    return hi, (v - hi.astype(F32)).astype(BF16)


def dot3(ah, al, bh, bl, dims):
    def one(a, b):
        return lax.dot_general(a, b, dims, preferred_element_type=F32)

    return one(ah, bh) + one(ah, bl) + one(al, bh)


def fold(v):
    lanes = v[:, 0:128]
    for k in range(1, v.shape[1] // 128):
        lanes = lanes + v[:, k * 128 : (k + 1) * 128]
    return jnp.sum(jnp.transpose(lanes), axis=0, keepdims=True)


def take(src, k, buf, hb, lb, sem, sq=None):
    pltpu.make_async_copy(src.at[0:R], buf.at[k], sem.at[k]).wait()
    for q in range(4):
        at = slice(q * 128, (q + 1) * 128)
        v = buf[k, at, :]
        hi, lo = split(v)
        hb[k, at, :] = hi
        lb[k, at, :] = lo
        if sq is not None:
            sq[k : k + 1, at] = fold(v * v)


def fetch(srcs, buf, sem):
    for k, src in enumerate(srcs):
        pltpu.make_async_copy(src.at[0:R], buf.at[k], sem.at[k]).start()


def near_kernel(meta, own, other, out4, out3, buf, hb, lb, ob, sq, sem, hsem, osem):
    del hsem
    fetch((own, other), buf, sem)
    sq[...] = jnp.zeros_like(sq)
    take(own, 0, buf, hb, lb, sem, sq)
    take(other, 1, buf, hb, lb, sem, sq)

    def copies(k, out):
        return [
            pltpu.make_async_copy(ob.at[k], out.at[0:R], osem.at[2 * k]),
            pltpu.make_async_copy(sq, out.at[R : R + 8], osem.at[2 * k + 1]),
        ]

    c4, c3 = copies(0, out4), copies(1, out3)

    @pl.when(meta[OWN_PAIR] == 1)
    def _():
        ob[0] = dot3(hb[0], lb[0], hb[0], lb[0], NT)
        start_all(c4)

    @pl.when(meta[ODD] == 1)
    def _():
        ob[1] = dot3(hb[1], lb[1], hb[0], lb[0], NT)
        start_all(c3)

    pl.when(meta[OWN_PAIR] == 1)(lambda: wait_all(c4))
    pl.when(meta[ODD] == 1)(lambda: wait_all(c3))


def far_a_kernel(meta, own, other, right, out, kh, kl, buf, hb, lb, ob, sq, sem, hsem, osem):
    del meta
    srcs = (right, own, other)
    fetch(srcs, buf, sem)
    sq[...] = jnp.zeros_like(sq)
    keep = []
    for k in range(3):
        take(srcs[k], k, buf, hb, lb, sem, sq)
        for j, (src, dst) in enumerate(((hb, kh), (lb, kl))):
            keep.append(pltpu.make_async_copy(src.at[k], dst.at[k], hsem.at[k, j]))
            keep[-1].start()
        if k:
            ob[k - 1] = dot3(hb[k], lb[k], hb[0], lb[0], NT)
            keep.append(pltpu.make_async_copy(ob.at[k - 1], out.at[(k - 1) * R : k * R], osem.at[k]))
            keep[-1].start()
    keep.append(pltpu.make_async_copy(sq, out.at[2 * R : 2 * R + 8], osem.at[0]))
    keep[-1].start()
    for c in keep:
        c.wait()


def far_b_kernel(meta, left, extra, right, out, out3, out5, kh, kl, buf, hb, lb, ob, sq, sem, hsem, osem):
    srcs = (left, extra, right)
    fetch(srcs, buf, sem)
    sq[...] = jnp.zeros_like(sq)
    keep = []
    for k in (2, 0):
        take(srcs[k], k, buf, hb, lb, sem, sq)
    ob[0] = dot3(hb[0], lb[0], hb[2], lb[2], NT)
    take(extra, 1, buf, hb, lb, sem, sq)
    keep.append(pltpu.make_async_copy(ob.at[0], out.at[0:R], osem.at[0]))
    keep.append(pltpu.make_async_copy(sq, out.at[R : R + 8], osem.at[3]))
    for k in range(2):
        for j, (src, dst) in enumerate(((hb, kh), (lb, kl))):
            keep.append(pltpu.make_async_copy(src.at[k], dst.at[k], hsem.at[k, j]))
    for c in keep:
        c.start()
    c3 = pltpu.make_async_copy(ob.at[1], out3, osem.at[1])
    c5 = pltpu.make_async_copy(ob.at[2], out5, osem.at[2])

    @pl.when(meta[EVEN] == 1)
    def _():
        ob[1] = dot3(hb[1], lb[1], hb[2], lb[2], NT)
        c3.start()

    @pl.when(meta[W_PAIR] == 1)
    def _():
        w = meta[W_RIGHT] * 2
        ob[2] = dot3(hb[w], lb[w], hb[w], lb[w], NT)
        c5.start()

    pl.when(meta[EVEN] == 1)(c3.wait)
    pl.when(meta[W_PAIR] == 1)(c5.wait)
    for c in keep:
        c.wait()


def scores_call(kernel, name, args, shapes, blocks, outs, squares):
    scratch = [
        pltpu.VMEM((blocks, R, F), F32),
        pltpu.VMEM((blocks, R, F), BF16),
        pltpu.VMEM((blocks, R, F), BF16),
        pltpu.VMEM((outs, R, R), F32),
    ]
    sems = [pltpu.SemaphoreType.DMA((blocks,))]
    if squares:
        scratch.append(pltpu.VMEM((8, R), F32))
        sems.append(pltpu.SemaphoreType.DMA((3, 2)))
    sems.append(pltpu.SemaphoreType.DMA((4,)))
    return pl.pallas_call(
        kernel,
        out_shape=shapes,
        in_specs=[SMEM_SPEC] + [ANY_SPEC] * (len(args) - 1),
        out_specs=[ANY_SPEC] * len(shapes),
        scratch_shapes=scratch + sems,
        compiler_params=PARAMS,
        cost_estimate=COST,
        name=name,
    )(*args)


def halves(n):
    return jax.ShapeDtypeStruct((n, R, F), BF16)


def sums_kernel(left, right, active, meta, mine, theirs, vec, s_out, t_out, p_out):
    part = pl.program_id(0)
    diag = left == right
    if left is None:
        left = right = meta[W_NAME]

    @pl.when(part == 0)
    def _():
        t_out[...] = jnp.zeros_like(t_out)
        p_out[...] = jnp.zeros_like(p_out)

    @pl.when(meta[active] == 1)
    def _():
        base_l, base_r = meta[BASE + left], meta[BASE + right]
        cols = jnp.transpose(vec[left])
        rows = lambda v: jnp.where(part == 0, v[0:H], v[H:R])
        inv_i = rows(cols[:, 0:1]) * 10.0
        part_i = rows(cols[:, 1:2]).astype(jnp.int32) - base_r
        inv_j = vec[right, 0:1, :]
        part_j = vec[right, 1:2, :].astype(jnp.int32) - base_l
        down = jnp.zeros((8, R), F32)
        down_n = jnp.zeros((8, R), F32)
        spos = jnp.zeros((8, R), F32)
        for k in range(H // 128):
            at = slice(k * 128, (k + 1) * 128)
            sc = (mine[at, :] + theirs[at, :]) * (inv_i[at] * inv_j)
            s_out[at, :] = sc
            r = lax.broadcasted_iota(jnp.int32, (128, R), 0) + (k * 128 + part * H)
            c = lax.broadcasted_iota(jnp.int32, (128, R), 1)
            ex = jnp.exp(sc - 10.0)
            if diag:
                ex = jnp.where(r == c, 0.0, ex)
            hits = part_i[at] == c
            back = part_j == r
            pos = jnp.where(hits, sc, 0.0)
            if not diag:
                pos += jnp.where(back, sc, 0.0)
            spos += jnp.sum(pos.reshape(16, 8, R), axis=0)
            here = pl.ds(pl.multiple_of(part * H + k * 128, 128), 128)
            t_out[left, 0:1, here] += fold(ex)
            t_out[left, 1:2, here] += fold(jnp.where(back, 1.0, 0.0))
            if not diag:
                down += jnp.sum(ex.reshape(16, 8, R), axis=0)
                down_n += jnp.sum(jnp.where(hits, 1.0, 0.0).reshape(16, 8, R), axis=0)
        if not diag:
            t_out[right, 0:1, :] += jnp.sum(down, axis=0, keepdims=True)
            t_out[right, 1:2, :] += jnp.sum(down_n, axis=0, keepdims=True)
        p_out[...] += spos


def pair_sums(meta, mine, theirs, vec, left, right, active=ALWAYS, first=0):
    cell = pl.BlockSpec((H, R), lambda g: (g + first, 0))
    return pl.pallas_call(
        functools.partial(sums_kernel, left, right, active),
        grid=(2,),
        out_shape=(MAT, jax.ShapeDtypeStruct((5, 8, R), F32), jax.ShapeDtypeStruct((8, R), F32)),
        in_specs=[SMEM_SPEC, cell, cell, pl.BlockSpec((5, 8, R), lambda g: (0, 0, 0))],
        out_specs=(
            pl.BlockSpec((H, R), lambda g: (g, 0)),
            pl.BlockSpec((5, 8, R), lambda g: (0, 0, 0)),
            pl.BlockSpec((8, R), lambda g: (0, 0)),
        ),
        compiler_params=pltpu.CompilerParams(vmem_limit_bytes=40 * 1024 * 1024),
        cost_estimate=pl.CostEstimate(flops=40 * R * R, bytes_accessed=12 * R * R, transcendentals=R * R),
        name="pair_sums",
    )(meta, mine, theirs, vec)


def coef_pair(left, right, diag, meta, sc_ref, vec, rbh, rbl, cbh, cbl, t_out):
    cols = jnp.transpose(vec[left])
    inv_i = cols[:, 0:1]
    part_i = cols[:, 1:2].astype(jnp.int32) - meta[BASE + right]
    a_i = cols[:, 2:3]
    inv_j = vec[right, 0:1, :]
    part_j = vec[right, 1:2, :].astype(jnp.int32) - meta[BASE + left]
    a_j = vec[right, 2:3, :]
    down = jnp.zeros((8, R), F32)
    for k in range(R // 128):
        at = slice(k * 128, (k + 1) * 128)
        sc = sc_ref[at, :]
        r = lax.broadcasted_iota(jnp.int32, (128, R), 0) + k * 128
        c = lax.broadcasted_iota(jnp.int32, (128, R), 1)
        ex = jnp.exp(sc - 10.0)
        if diag:
            ex = jnp.where(r == c, 0.0, ex)
        cf = ex * (a_i[at] + a_j)
        cf = jnp.where(part_i[at] == c, cf - 1.0, cf)
        cf = jnp.where(part_j == r, cf - 1.0, cf)
        pr = cf * sc
        t_out[left, 0:1, at] += fold(pr)
        hi, lo = split(cf * inv_j)
        rbh[at, :] = hi
        rbl[at, :] = lo
        if not diag:
            down += jnp.sum(pr.reshape(16, 8, R), axis=0)
            hi, lo = split(cf * inv_i[at])
            cbh[at, :] = hi
            cbl[at, :] = lo
    if not diag:
        t_out[right, 0:1, :] += jnp.sum(down, axis=0, keepdims=True)


def start_all(copies):
    for c in copies:
        c.start()


def wait_all(copies):
    for c in copies:
        c.wait()


def coef_a_kernel(meta, s2, s3e, s3o, s5, vec, kh, kl, meh, mel, rh, rl, ch, cl, m_out, y_out, t_out,
                  sbuf, rbh, rbl, cbh, cbl, uh, ul, wh, wl, ssem, usem, wsem, csem):
    even = meta[PAR] == 0
    loads = [pltpu.make_async_copy(s2, sbuf.at[k], ssem.at[k]) for k in range(3)]

    @pl.when(even)
    def _():
        pltpu.make_async_copy(s3e, sbuf.at[1], ssem.at[1]).start()

    @pl.when(jnp.logical_not(even))
    def _():
        pltpu.make_async_copy(s3o, sbuf.at[1], ssem.at[1]).start()

    loads[0].start()
    units = [pltpu.make_async_copy(src.at[k], dst.at[k], usem.at[k, j]) for k in (0, 1) for j, (src, dst) in enumerate(((kh, uh), (kl, ul)))]
    start_all(units)
    wpair = jnp.logical_and(meta[W_PAIR] == 1, meta[W_RIGHT] == 0)
    wcopies = [pltpu.make_async_copy(src.at[0], dst, wsem.at[j]) for j, (src, dst) in enumerate(((meh, wh), (mel, wl)))]
    pl.when(wpair)(lambda: start_all(wcopies))

    @pl.when(meta[W_PAIR] == 1)
    def _():
        pltpu.make_async_copy(s5, sbuf.at[2], ssem.at[2]).start()

    t_out[...] = jnp.zeros_like(t_out)

    def outs(k):
        out = [pltpu.make_async_copy(rbh.at[k], rh.at[k], csem.at[k, 0]), pltpu.make_async_copy(rbl.at[k], rl.at[k], csem.at[k, 1])]
        if k < 2:
            out += [pltpu.make_async_copy(cbh.at[k], ch.at[k], csem.at[k, 2]), pltpu.make_async_copy(cbl.at[k], cl.at[k], csem.at[k, 3])]
        return out

    loads[1].wait()
    left = jnp.where(even, E, X)
    right = jnp.where(even, N, O)
    coef_pair(left, right, False, meta, sbuf.at[1], vec, rbh.at[1], rbl.at[1], cbh.at[1], cbl.at[1], t_out)
    start_all(outs(1))
    loads[0].wait()
    coef_pair(M, N, False, meta, sbuf.at[0], vec, rbh.at[0], rbl.at[0], cbh.at[0], cbl.at[0], t_out)
    start_all(outs(0))
    wait_all(units)
    y_out[0:R, :] = dot3(rbh[1], rbl[1], uh[meta[PAR]], ul[meta[PAR]], NN)
    m_out[0:R, :] = dot3(rbh[0], rbl[0], uh[0], ul[0], NN)

    @pl.when(meta[W_PAIR] == 1)
    def _():
        loads[2].wait()
        w = meta[W_NAME]
        coef_pair(w, w, True, meta, sbuf.at[2], vec, rbh.at[2], rbl.at[2], None, None, t_out)
        start_all(outs(2))

    @pl.when(wpair)
    def _():
        wait_all(wcopies)
        m_out[0:R, :] += dot3(rbh[2], rbl[2], wh[...], wl[...], NN)

    m_out[R : R + 8, 0:R] = t_out[M]
    y_out[R : R + 8, 0:R] = t_out[E]
    pl.when(meta[W_PAIR] == 1)(lambda: wait_all(outs(2)))
    wait_all(outs(0) + outs(1))


def coef_a(meta, scores, vec, k_halves, me_halves):
    half = lambda n: jax.ShapeDtypeStruct((n, R, R), BF16)
    return pl.pallas_call(
        coef_a_kernel,
        out_shape=(half(3), half(3), half(2), half(2), WHOLE, WHOLE, jax.ShapeDtypeStruct((5, 8, R), F32)),
        in_specs=[SMEM_SPEC] + [ANY_SPEC] * 4 + [FULL] + [ANY_SPEC] * 4,
        out_specs=(ANY_SPEC,) * 4 + (FULL,) * 3,
        scratch_shapes=[
            pltpu.VMEM((3, R, R), F32),
            pltpu.VMEM((3, R, R), BF16),
            pltpu.VMEM((3, R, R), BF16),
            pltpu.VMEM((2, R, R), BF16),
            pltpu.VMEM((2, R, R), BF16),
            pltpu.VMEM((2, R, F), BF16),
            pltpu.VMEM((2, R, F), BF16),
            pltpu.VMEM((R, F), BF16),
            pltpu.VMEM((R, F), BF16),
            pltpu.SemaphoreType.DMA((3,)),
            pltpu.SemaphoreType.DMA((2, 2)),
            pltpu.SemaphoreType.DMA((2,)),
            pltpu.SemaphoreType.DMA((3, 4)),
        ],
        compiler_params=PARAMS,
        cost_estimate=COST,
        name="coef_a",
    )(meta, *scores, vec, *k_halves, *me_halves)


def coef_b_kernel(meta, s0, s1, vec, nh, nl, ta, rh, rl, ch, cl, t_out, x_out):
    k = pl.program_id(0)

    @pl.when(k == 0)
    def _():
        t_out[...] = jnp.zeros_like(t_out)
        coef_pair(O, N, False, meta, s0, vec, rh.at[0], rl.at[0], ch.at[0], cl.at[0], t_out)

    @pl.when(k == 1)
    def _():
        coef_pair(X, N, False, meta, s1, vec, rh.at[0], rl.at[0], ch.at[0], cl.at[0], t_out)
        x_out[0:R, :] = dot3(rh[0], rl[0], nh[0], nl[0], NN)
        x_out[R : R + 8, 0:R] = ta[X] + t_out[X]


def coef_b(meta, s0, s1, vec, units, ta):
    half = jax.ShapeDtypeStruct((2, R, R), BF16)
    one = pl.BlockSpec((1, R, R), lambda k: (k, 0, 0))
    mat = pl.BlockSpec((R, R), lambda k: (0, 0))
    stay = pl.BlockSpec((5, 8, R), lambda k: (0, 0, 0))
    unit = pl.BlockSpec((1, R, F), lambda k: (0, 0, 0))
    return pl.pallas_call(
        coef_b_kernel,
        grid=(2,),
        out_shape=(half,) * 4 + (jax.ShapeDtypeStruct((5, 8, R), F32), WHOLE),
        in_specs=[SMEM_SPEC, mat, mat, stay, unit, unit, stay],
        out_specs=(one,) * 4 + (stay, pl.BlockSpec((R + 8, F), lambda k: (0, 0))),
        compiler_params=PARAMS,
        cost_estimate=COST,
        name="coef_b",
    )(meta, s0, s1, vec, *units, ta)


def right_kernel(part, meta, chb, clb, cha, cla, rha, rla, kh, kl, meh, mel, ta, tb, *refs):
    if part == 0:
        m, swap, out, left, cbh, cbl, ubh, ubl, mbuf, wbuf, sem, msem = refs
        mcopies = [pltpu.make_async_copy(src, dst, msem.at[k]) for k, (src, dst) in enumerate(((m, mbuf), (swap, wbuf)))]
        l_copy = pltpu.make_async_copy(mbuf, left, msem.at[2])
    else:
        out, cbh, cbl, ubh, ubl, sem = refs
    at = pl.ds(part * (F // 2), F // 2)
    terms = (
        (chb.at[0], clb.at[0], kh.at[1, :, at], kl.at[1, :, at]),
        (chb.at[1], clb.at[1], kh.at[2, :, at], kl.at[2, :, at]),
        (cha.at[0], cla.at[0], meh.at[0, :, at], mel.at[0, :, at]),
        (cha.at[1], cla.at[1], meh.at[1, :, at], mel.at[1, :, at]),
        (rha.at[2], rla.at[2], kh.at[0, :, at], kl.at[0, :, at]),
    )

    def copies(t):
        return [pltpu.make_async_copy(src, dst.at[t], sem.at[t, j]) for j, (src, dst) in enumerate(zip(terms[t], (cbh, cbl, ubh, ubl)))]

    def term(t):
        wait_all(copies(t))
        v = dot3(cbh[t], cbl[t], ubh[t], ubl[t], NN if t == 4 else TN)
        if t == 0:
            out[0:R, :] = v
        else:
            out[0:R, :] += v

    even = meta[EVEN] == 1
    wright = jnp.logical_and(meta[W_PAIR] == 1, meta[W_RIGHT] == 1)
    for t in range(3):
        start_all(copies(t))
    pl.when(even)(lambda: start_all(copies(3)))
    pl.when(wright)(lambda: start_all(copies(4)))
    if part == 0:
        start_all(mcopies)
        out[R : R + 8, 0:R] = ta[N] + tb[N]
    term(0)
    if part == 0:
        wait_all(mcopies)

        @pl.when(jnp.logical_not(even))
        def _():
            mbuf[...] += wbuf[...]

        l_copy.start()
    term(1)
    term(2)
    pl.when(even)(lambda: term(3))
    pl.when(wright)(lambda: term(4))
    if part == 0:
        l_copy.wait()


def right_part(part, meta, mats, units, ta, tb, more=()):
    thin = jax.ShapeDtypeStruct((R + 8 * (1 - part), F // 2), F32)
    return pl.pallas_call(
        functools.partial(right_kernel, part),
        out_shape=thin if part else (thin, WHOLE),
        in_specs=[SMEM_SPEC] + [ANY_SPEC] * 10 + [FULL] * 2 + [ANY_SPEC] * len(more),
        out_specs=FULL if part else (FULL, ANY_SPEC),
        scratch_shapes=[
            pltpu.VMEM((5, R, R), BF16),
            pltpu.VMEM((5, R, R), BF16),
            pltpu.VMEM((5, R, F // 2), BF16),
            pltpu.VMEM((5, R, F // 2), BF16),
        ]
        + [pltpu.VMEM((R + 8, F), F32)] * len(more)
        + [pltpu.SemaphoreType.DMA((5, 4))]
        + [pltpu.SemaphoreType.DMA((3,))] * (len(more) // 2),
        compiler_params=PARAMS,
        cost_estimate=COST,
        name="right_part",
    )(meta, *mats, *units, ta, tb, *more)


def own_kernel(meta, s4, rhb, rlb, cha, cla, kh, kl, vec, ta, tb, more, swap, out, sbuf, cbh, cbl, ubh, ubl, t, mbuf, ssem, csem, usem, msem):
    odd = meta[ODD] == 1
    pair = meta[OWN_PAIR] == 1
    load = pltpu.make_async_copy(s4, sbuf, ssem)
    pl.when(pair)(load.start)
    units = [pltpu.make_async_copy(src.at[k], dst.at[k], usem.at[k, j]) for k in range(3) for j, (src, dst) in enumerate(((kh, ubh), (kl, ubl)))]
    mats = [pltpu.make_async_copy(src.at[0], dst.at[0], csem.at[0, j]) for j, (src, dst) in enumerate(((rhb, cbh), (rlb, cbl)))]
    mats += [pltpu.make_async_copy(src.at[1], dst.at[1], csem.at[1, j]) for j, (src, dst) in enumerate(((cha, cbh), (cla, cbl)))]
    start_all(units + mats)
    adds = [pltpu.make_async_copy(src, mbuf.at[j], msem.at[j]) for j, src in enumerate((more, swap))]
    start_all(adds)
    t[...] = ta[...] + tb[...]
    wait_all(units + mats)
    out[0:R, :] = dot3(cbh[0], cbl[0], ubh[0], ubl[0], NN)

    @pl.when(odd)
    def _():
        out[0:R, :] += dot3(cbh[1], cbl[1], ubh[2], ubl[2], TN)

    @pl.when(pair)
    def _():
        load.wait()
        coef_pair(O, O, True, meta, sbuf, vec, cbh.at[2], cbl.at[2], None, None, t)
        out[0:R, :] += dot3(cbh[2], cbl[2], ubh[1], ubl[1], NN)

    out[R : R + 8, 0:R] = t[O]
    wait_all(adds)
    out[...] += mbuf[0]

    @pl.when(jnp.logical_not(odd))
    def _():
        out[...] += mbuf[1]


def own_part(meta, s4, rows, cols, units, vec, ta, tb, more, swap):
    return pl.pallas_call(
        own_kernel,
        out_shape=WHOLE,
        in_specs=[SMEM_SPEC] + [ANY_SPEC] * 7 + [FULL] * 3 + [ANY_SPEC] * 2,
        out_specs=FULL,
        scratch_shapes=[
            pltpu.VMEM((R, R), F32),
            pltpu.VMEM((3, R, R), BF16),
            pltpu.VMEM((3, R, R), BF16),
            pltpu.VMEM((3, R, F), BF16),
            pltpu.VMEM((3, R, F), BF16),
            pltpu.VMEM((5, 8, R), F32),
            pltpu.VMEM((2, R + 8, F), F32),
            pltpu.SemaphoreType.DMA,
            pltpu.SemaphoreType.DMA((2, 2)),
            pltpu.SemaphoreType.DMA((3, 2)),
            pltpu.SemaphoreType.DMA((2,)),
        ],
        compiler_params=PARAMS,
        cost_estimate=COST,
        name="own_part",
    )(meta, s4, *rows, *cols, *units, vec, ta, tb, more, swap)


def grads_kernel(right, left, left2, own, kept, vec, out, rb, lb, l2b, ob, kb, gb, sem, tsem):
    T = 128
    chunks = [slice(k * T, (k + 1) * T) for k in range(R // T)]
    srcs = ((right, rb), (left, lb), (left2, l2b), (own, ob), (kept, kb))
    tails = [pltpu.make_async_copy(src.at[R : R + 8], dst.at[R : R + 8], tsem.at[k]) for k, (src, dst) in enumerate(((right, rb), (left, lb), (kept, kb)))]
    start_all(tails)
    loads = [[pltpu.make_async_copy(src.at[at], dst.at[at], sem.at[k, j]) for j, (src, dst) in enumerate(srcs)] for k, at in enumerate(chunks)]
    stores = [pltpu.make_async_copy(gb.at[at], out.at[at], sem.at[k, 5]) for k, at in enumerate(chunks)]
    for load in loads:
        start_all(load)
    wait_all(tails)
    along = jnp.transpose(rb[R : R + 8, 0:R] + lb[R : R + 8, 0:R] + kb[R : R + 8, 0:R])[:, 0:1]
    inv = jnp.transpose(vec[O])[:, 0:1]
    scale = inv * along
    for k, at in enumerate(chunks):
        wait_all(loads[k])
        for part, cols in ((lb, slice(0, F // 2)), (l2b, slice(F // 2, F))):
            grad = kb[at, cols] + rb[at, cols] + part[at, :]
            gb[at, cols] = (grad * 10.0 - ob[at, cols] * scale[at]) * inv[at]
        stores[k].start()
    wait_all(stores)


def grads_of(kept, right, left, left2, own, vec):
    return pl.pallas_call(
        grads_kernel,
        out_shape=jax.ShapeDtypeStruct((R, F), F32),
        in_specs=[ANY_SPEC] * 5 + [FULL],
        out_specs=ANY_SPEC,
        scratch_shapes=[
            pltpu.VMEM((R + 8, F), F32),
            pltpu.VMEM((R + 8, F // 2), F32),
            pltpu.VMEM((R, F // 2), F32),
            pltpu.VMEM((R, F), F32),
            pltpu.VMEM((R + 8, F), F32),
            pltpu.VMEM((R, F), F32),
            pltpu.SemaphoreType.DMA((4, 6)),
            pltpu.SemaphoreType.DMA((3,)),
        ],
        compiler_params=pltpu.CompilerParams(vmem_limit_bytes=20 * 1024 * 1024),
        name="grads",
    )(right, left, left2, own, kept, vec)


def per_device(embeddings, partner):
    blk = lax.axis_index("blk")
    count = lax.axis_size("blk")
    par = (blk % 2).astype(jnp.int32)
    even = par == 0
    row = (blk // 2) % 4
    inner = jnp.logical_or(row == 1, row == 2)

    def is_inner(i):
        return (i // 2) % 4 in (1, 2)

    def shift(v, steps):
        return lax.ppermute(v, "blk", [(i, (i + steps) % count) for i in range(count)])

    def cores(v):
        return lax.ppermute(v, "blk", [(i, i ^ 1) for i in range(count)])

    def outwards(v):
        return lax.ppermute(v, "blk", [(i, (i + (2 if i % 2 else -2)) % count) for i in range(count)])

    def feats(v, where=None):
        if where is None:
            return lax.ppermute(v, "feat", [(0, 1), (1, 0)])
        pairs = [(2 * i + f, 2 * i + 1 - f) for i in range(count) if where(i) for f in (0, 1)]
        return lax.ppermute(v, ("blk", "feat"), pairs)

    own = embeddings
    line = jnp.pad(partner.astype(F32)[None], ((0, 7), (0, F - R)))
    block = jnp.concatenate([own, line], axis=0)
    right = shift(block, -2)
    left = shift(block, 2)
    other = cores(block)
    names = jnp.stack([blk + count - 2, blk + count - 1, blk, blk + 1 - 2 * par, blk + 2]) % count
    own_pair = jnp.logical_or(inner, par == 1).astype(jnp.int32)
    w_pair = jnp.logical_and(inner, par == 0).astype(jnp.int32)
    w_right = (row == 2).astype(jnp.int32)
    flags = jnp.stack([own_pair, w_pair, w_right * N, w_right, 1 - par, par, jnp.ones_like(par)])
    meta = jnp.concatenate([par[None], names.astype(jnp.int32) * R, flags.astype(jnp.int32)])

    s_rows = lambda n: jax.ShapeDtypeStruct((n * R + 8, R), F32)
    own_pairs = lambda i: i % 2 == 1 or is_inner(i)
    w_pairs = lambda i: i % 2 == 0 and is_inner(i)
    p4, p3o = scores_call(near_kernel, "near_scores", (meta, block, other), (s_rows(1), s_rows(1)), 2, 2, True)
    g4, g3o = feats(p4, own_pairs), feats(p3o, lambda i: i % 2 == 1)
    extra = lax.ppermute(left, "blk", [(i + 1, i) for i in range(0, count, 2)])
    right, g4, g3o = lax.optimization_barrier((right, g4, g3o))
    far, kh, kl = scores_call(
        far_a_kernel, "far_scores_a", (meta, block, other, right), (s_rows(2), halves(3), halves(3)), 3, 2, True
    )
    far_g = feats(far)
    left, extra, kh = lax.optimization_barrier((left, extra, kh))
    p2, p3e, p5, meh, mel = scores_call(
        far_b_kernel, "far_scores_b", (meta, left, extra, right), (s_rows(1), MAT, MAT, halves(2), halves(2)), 3, 3, True
    )
    g2, g3e, g5 = feats(p2), feats(p3e, lambda i: i % 2 == 0), feats(p5, w_pairs)

    def inverse(mine, theirs):
        return 1.0 / jnp.sqrt(mine + theirs + 1e-06)

    def vectors(cells):
        zero = jnp.zeros((R,), F32)
        return jnp.stack([jnp.stack(c + [zero] * (8 - len(c))) for c in cells])

    who = lambda b: b[R, 0:R]
    inv_nox = inverse(far[2 * R : 2 * R + 3], far_g[2 * R : 2 * R + 3])
    inv_me = inverse(p2[R : R + 2], g2[R : R + 2])
    packs = [
        [inv_me[0], who(left)],
        [inv_me[1], who(extra)],
        [inv_nox[1], who(block)],
        [inv_nox[2], who(other)],
        [inv_nox[0], who(right)],
    ]
    vec_a = vectors([[], []] + packs[2:])
    near_inv = jnp.where(even, inverse(p4[R : R + 2], g4[R : R + 2]), inverse(p3o[R : R + 2], g3o[R : R + 2]))
    vec_near = vectors([[], [], [near_inv[0], who(block)], [near_inv[1], who(other)], []])
    sums = []

    def pair(*args, **kw):
        s, t, p = pair_sums(meta, *args, **kw)
        sums.append((t[:, 0:2], p))
        return s

    s4 = pair(p4, g4, vec_near, O, O, active=OWN_PAIR)
    s3o = pair(p3o, g3o, vec_near, X, O, active=ODD)
    s0 = pair(far, far_g, vec_a, O, N)
    s1 = pair(far, far_g, vec_a, X, N, first=2)
    vec_b = vectors(packs)
    s3e = pair(p3e, g3e, vec_b, E, N, active=EVEN)
    s5 = pair(p5, g5, vec_b, None, None, active=W_PAIR)
    s2 = pair(p2, g2, vec_b, M, N)

    t = sum(v for v, _ in sums)
    p = jnp.sum(sum(v for _, v in sums), axis=0)
    zero = jnp.zeros((2, R), F32)
    spos = jnp.stack([p, p * 0.0])
    chip = jnp.where(
        even, jnp.stack([t[M], t[E], t[O], t[X], t[N], zero, spos]), jnp.stack([zero, t[M], t[X], t[O], zero, t[N], spos])
    )
    chip = chip + cores(chip)
    got = outwards(jnp.where(even, chip[0:2], chip[4:6]))
    total = chip[2:4] + (got + cores(got))
    counts = total[:, 1] + 1.0
    a = counts * 0.5 / total[:, 0]
    loss = jnp.sum(counts * (10.0 + jnp.log(total[:, 0]))) * 0.5 - jnp.sum(chip[6, 0])
    a_one = outwards(jnp.concatenate([a, jnp.full((1, R), loss, F32)], axis=0))
    a_two = cores(a_one)
    a_l, a_r = jnp.where(even, a_two, a_one), jnp.where(even, a_one, a_two)
    mine = lambda v: jnp.where(even, v[0], v[1])
    a_all = [mine(a_l), a_l[1], mine(a), mine(a[::-1]), mine(a_r)]
    vec = vectors([p + [q] for p, q in zip(packs, a_all)])
    loss = loss + jnp.where(row % 2 == 0, a_r[2, 0], a_l[2, 0])

    def both(v, k):
        return v + lax.ppermute(v, "blk", [(i, i ^ k) for i in range(count)])

    rha, rla, cha, cla, to_left, swap, ta = coef_a(meta, (s2, s3e, s3o, s5), vec, (kh, kl), (meh, mel))
    swapped = cores(swap)
    vec, ta = lax.optimization_barrier((vec, ta))
    rhb, rlb, chb, clb, tb, to_other = coef_b(meta, s0, s1, vec, (kh, kl), ta)
    loss = both(loss, 4)
    tb, loss = lax.optimization_barrier((tb, loss))
    mats, units = (chb, clb, cha, cla, rha, rla), (kh, kl, meh, mel)
    to_right, to_left = right_part(0, meta, mats, units, ta, tb, (to_left, swapped))
    from_right = shift(to_left, -2)
    from_left = shift(to_right, 2)
    clb, to_right = lax.optimization_barrier((clb, to_right))
    mats = (chb, clb, cha, cla, rha, rla)
    to_right_2 = right_part(1, meta, mats, units, ta, tb)
    from_left_2 = shift(to_right_2, 2)
    loss, to_right_2 = lax.optimization_barrier((loss, to_right_2))
    from_other = cores(to_other)
    loss = both(both(loss, 16), 32)
    loss, rhb = lax.optimization_barrier((loss, rhb))
    kept = own_part(meta, s4, (rhb, rlb), (cha, cla), (kh, kl), vec, ta, tb, from_other, swapped)
    loss, kept = lax.optimization_barrier((loss, kept))
    loss = both(loss, 8) / (count * R)
    grads = grads_of(kept, from_right, from_left, from_left_2, own, vec)
    grads, loss = lax.optimization_barrier((grads, loss))
    return (loss, grads)


def solution(mesh):
    in_specs = (P("blk", "feat"), P("blk"))
    out_specs = (P(), P("blk", "feat"))
    return jax.shard_map(per_device, mesh=mesh, in_specs=in_specs, out_specs=out_specs, check_vma=False)
```

```python
import functools

import jax
import jax.numpy as jnp
from jax import lax
from jax.experimental import pallas as pl
from jax.experimental.pallas import tpu as pltpu
from jax.sharding import PartitionSpec as P

R = 512
H = 256
F = 1024
F32 = jnp.float32
BF16 = jnp.bfloat16
NT = (((1,), (1,)), ((), ()))
NN = (((1,), (0,)), ((), ()))
TN = (((0,), (0,)), ((), ()))
M, E, O, X, N = range(5)
PAR, BASE, OWN_PAIR, W_PAIR, W_NAME, W_RIGHT, EVEN, ODD, ALWAYS = 0, 1, 6, 7, 8, 9, 10, 11, 12
SMEM_SPEC = pl.BlockSpec(memory_space=pltpu.SMEM)
ANY_SPEC = pl.BlockSpec(memory_space=pl.ANY)
FULL = pl.BlockSpec(memory_space=pltpu.VMEM)
PARAMS = pltpu.CompilerParams(vmem_limit_bytes=56 * 1024 * 1024)
COST = pl.CostEstimate(flops=12 * R * R * F, bytes_accessed=8 * R * F * 4, transcendentals=0)
WHOLE = jax.ShapeDtypeStruct((R + 8, F), F32)
MAT = jax.ShapeDtypeStruct((R, R), F32)


def split(v):
    hi = v.astype(BF16)
    return hi, (v - hi.astype(F32)).astype(BF16)


def dot3(ah, al, bh, bl, dims):
    def one(a, b):
        return lax.dot_general(a, b, dims, preferred_element_type=F32)

    return one(ah, bh) + one(ah, bl) + one(al, bh)


def fold(v):
    lanes = v[:, 0:128]
    for k in range(1, v.shape[1] // 128):
        lanes = lanes + v[:, k * 128 : (k + 1) * 128]
    return jnp.sum(jnp.transpose(lanes), axis=0, keepdims=True)


def take(src, k, buf, hb, lb, sem, sq=None):
    pltpu.make_async_copy(src.at[0:R], buf.at[k], sem.at[k]).wait()
    for q in range(4):
        at = slice(q * 128, (q + 1) * 128)
        v = buf[k, at, :]
        hi, lo = split(v)
        hb[k, at, :] = hi
        lb[k, at, :] = lo
        if sq is not None:
            sq[k : k + 1, at] = fold(v * v)


def fetch(srcs, buf, sem):
    for k, src in enumerate(srcs):
        pltpu.make_async_copy(src.at[0:R], buf.at[k], sem.at[k]).start()


def near_kernel(meta, own, other, out4, out3, buf, hb, lb, ob, sq, sem, hsem, osem):
    del hsem
    fetch((own, other), buf, sem)
    sq[...] = jnp.zeros_like(sq)
    take(own, 0, buf, hb, lb, sem, sq)
    take(other, 1, buf, hb, lb, sem, sq)

    def copies(k, out):
        return [
            pltpu.make_async_copy(ob.at[k], out.at[0:R], osem.at[2 * k]),
            pltpu.make_async_copy(sq, out.at[R : R + 8], osem.at[2 * k + 1]),
        ]

    c4, c3 = copies(0, out4), copies(1, out3)

    @pl.when(meta[OWN_PAIR] == 1)
    def _():
        ob[0] = dot3(hb[0], lb[0], hb[0], lb[0], NT)
        start_all(c4)

    @pl.when(meta[ODD] == 1)
    def _():
        ob[1] = dot3(hb[1], lb[1], hb[0], lb[0], NT)
        start_all(c3)

    pl.when(meta[OWN_PAIR] == 1)(lambda: wait_all(c4))
    pl.when(meta[ODD] == 1)(lambda: wait_all(c3))


def far_a_kernel(meta, own, other, right, out, kh, kl, buf, hb, lb, ob, sq, sem, hsem, osem):
    del meta
    srcs = (right, own, other)
    fetch(srcs, buf, sem)
    sq[...] = jnp.zeros_like(sq)
    keep = []
    for k in range(3):
        take(srcs[k], k, buf, hb, lb, sem, sq)
        for j, (src, dst) in enumerate(((hb, kh), (lb, kl))):
            keep.append(pltpu.make_async_copy(src.at[k], dst.at[k], hsem.at[k, j]))
            keep[-1].start()
        if k:
            ob[k - 1] = dot3(hb[k], lb[k], hb[0], lb[0], NT)
            keep.append(pltpu.make_async_copy(ob.at[k - 1], out.at[(k - 1) * R : k * R], osem.at[k]))
            keep[-1].start()
    keep.append(pltpu.make_async_copy(sq, out.at[2 * R : 2 * R + 8], osem.at[0]))
    keep[-1].start()
    for c in keep:
        c.wait()


def far_b_kernel(meta, left, extra, right, out, out3, out5, kh, kl, buf, hb, lb, ob, sq, sem, hsem, osem):
    srcs = (left, extra, right)
    fetch(srcs, buf, sem)
    sq[...] = jnp.zeros_like(sq)
    keep = []
    for k in (2, 0):
        take(srcs[k], k, buf, hb, lb, sem, sq)
    ob[0] = dot3(hb[0], lb[0], hb[2], lb[2], NT)
    take(extra, 1, buf, hb, lb, sem, sq)
    keep.append(pltpu.make_async_copy(ob.at[0], out.at[0:R], osem.at[0]))
    keep.append(pltpu.make_async_copy(sq, out.at[R : R + 8], osem.at[3]))
    for k in range(2):
        for j, (src, dst) in enumerate(((hb, kh), (lb, kl))):
            keep.append(pltpu.make_async_copy(src.at[k], dst.at[k], hsem.at[k, j]))
    for c in keep:
        c.start()
    c3 = pltpu.make_async_copy(ob.at[1], out3, osem.at[1])
    c5 = pltpu.make_async_copy(ob.at[2], out5, osem.at[2])

    @pl.when(meta[EVEN] == 1)
    def _():
        ob[1] = dot3(hb[1], lb[1], hb[2], lb[2], NT)
        c3.start()

    @pl.when(meta[W_PAIR] == 1)
    def _():
        w = meta[W_RIGHT] * 2
        ob[2] = dot3(hb[w], lb[w], hb[w], lb[w], NT)
        c5.start()

    pl.when(meta[EVEN] == 1)(c3.wait)
    pl.when(meta[W_PAIR] == 1)(c5.wait)
    for c in keep:
        c.wait()


def scores_call(kernel, name, args, shapes, blocks, outs, squares):
    scratch = [
        pltpu.VMEM((blocks, R, F), F32),
        pltpu.VMEM((blocks, R, F), BF16),
        pltpu.VMEM((blocks, R, F), BF16),
        pltpu.VMEM((outs, R, R), F32),
    ]
    sems = [pltpu.SemaphoreType.DMA((blocks,))]
    if squares:
        scratch.append(pltpu.VMEM((8, R), F32))
        sems.append(pltpu.SemaphoreType.DMA((3, 2)))
    sems.append(pltpu.SemaphoreType.DMA((4,)))
    return pl.pallas_call(
        kernel,
        out_shape=shapes,
        in_specs=[SMEM_SPEC] + [ANY_SPEC] * (len(args) - 1),
        out_specs=[ANY_SPEC] * len(shapes),
        scratch_shapes=scratch + sems,
        compiler_params=PARAMS,
        cost_estimate=COST,
        name=name,
    )(*args)


def halves(n):
    return jax.ShapeDtypeStruct((n, R, F), BF16)


def sums_kernel(left, right, active, meta, mine, theirs, vec, s_out, t_out, p_out):
    part = pl.program_id(0)
    diag = left == right
    if left is None:
        left = right = meta[W_NAME]

    @pl.when(part == 0)
    def _():
        t_out[...] = jnp.zeros_like(t_out)
        p_out[...] = jnp.zeros_like(p_out)

    @pl.when(meta[active] == 1)
    def _():
        base_l, base_r = meta[BASE + left], meta[BASE + right]
        cols = jnp.transpose(vec[left])
        rows = lambda v: jnp.where(part == 0, v[0:H], v[H:R])
        inv_i = rows(cols[:, 0:1]) * 10.0
        part_i = rows(cols[:, 1:2]).astype(jnp.int32) - base_r
        inv_j = vec[right, 0:1, :]
        part_j = vec[right, 1:2, :].astype(jnp.int32) - base_l
        down = jnp.zeros((8, R), F32)
        down_n = jnp.zeros((8, R), F32)
        spos = jnp.zeros((8, R), F32)
        for k in range(H // 128):
            at = slice(k * 128, (k + 1) * 128)
            sc = (mine[at, :] + theirs[at, :]) * (inv_i[at] * inv_j)
            s_out[at, :] = sc
            r = lax.broadcasted_iota(jnp.int32, (128, R), 0) + (k * 128 + part * H)
            c = lax.broadcasted_iota(jnp.int32, (128, R), 1)
            ex = jnp.exp(sc - 10.0)
            if diag:
                ex = jnp.where(r == c, 0.0, ex)
            hits = part_i[at] == c
            back = part_j == r
            pos = jnp.where(hits, sc, 0.0)
            if not diag:
                pos += jnp.where(back, sc, 0.0)
            spos += jnp.sum(pos.reshape(16, 8, R), axis=0)
            here = pl.ds(pl.multiple_of(part * H + k * 128, 128), 128)
            t_out[left, 0:1, here] += fold(ex)
            t_out[left, 1:2, here] += fold(jnp.where(back, 1.0, 0.0))
            if not diag:
                down += jnp.sum(ex.reshape(16, 8, R), axis=0)
                down_n += jnp.sum(jnp.where(hits, 1.0, 0.0).reshape(16, 8, R), axis=0)
        if not diag:
            t_out[right, 0:1, :] += jnp.sum(down, axis=0, keepdims=True)
            t_out[right, 1:2, :] += jnp.sum(down_n, axis=0, keepdims=True)
        p_out[...] += spos


def pair_sums(meta, mine, theirs, vec, left, right, active=ALWAYS, first=0):
    cell = pl.BlockSpec((H, R), lambda g: (g + first, 0))
    return pl.pallas_call(
        functools.partial(sums_kernel, left, right, active),
        grid=(2,),
        out_shape=(MAT, jax.ShapeDtypeStruct((5, 8, R), F32), jax.ShapeDtypeStruct((8, R), F32)),
        in_specs=[SMEM_SPEC, cell, cell, pl.BlockSpec((5, 8, R), lambda g: (0, 0, 0))],
        out_specs=(
            pl.BlockSpec((H, R), lambda g: (g, 0)),
            pl.BlockSpec((5, 8, R), lambda g: (0, 0, 0)),
            pl.BlockSpec((8, R), lambda g: (0, 0)),
        ),
        compiler_params=pltpu.CompilerParams(vmem_limit_bytes=40 * 1024 * 1024),
        cost_estimate=pl.CostEstimate(flops=40 * R * R, bytes_accessed=12 * R * R, transcendentals=R * R),
        name="pair_sums",
    )(meta, mine, theirs, vec)


def coef_pair(left, right, diag, meta, sc_ref, vec, rbh, rbl, cbh, cbl, t_out):
    cols = jnp.transpose(vec[left])
    inv_i = cols[:, 0:1]
    part_i = cols[:, 1:2].astype(jnp.int32) - meta[BASE + right]
    a_i = cols[:, 2:3]
    inv_j = vec[right, 0:1, :]
    part_j = vec[right, 1:2, :].astype(jnp.int32) - meta[BASE + left]
    a_j = vec[right, 2:3, :]
    down = jnp.zeros((8, R), F32)
    for k in range(R // 128):
        at = slice(k * 128, (k + 1) * 128)
        sc = sc_ref[at, :]
        r = lax.broadcasted_iota(jnp.int32, (128, R), 0) + k * 128
        c = lax.broadcasted_iota(jnp.int32, (128, R), 1)
        ex = jnp.exp(sc - 10.0)
        if diag:
            ex = jnp.where(r == c, 0.0, ex)
        cf = ex * (a_i[at] + a_j)
        cf = jnp.where(part_i[at] == c, cf - 1.0, cf)
        cf = jnp.where(part_j == r, cf - 1.0, cf)
        pr = cf * sc
        t_out[left, 0:1, at] += fold(pr)
        hi, lo = split(cf * inv_j)
        rbh[at, :] = hi
        rbl[at, :] = lo
        if not diag:
            down += jnp.sum(pr.reshape(16, 8, R), axis=0)
            hi, lo = split(cf * inv_i[at])
            cbh[at, :] = hi
            cbl[at, :] = lo
    if not diag:
        t_out[right, 0:1, :] += jnp.sum(down, axis=0, keepdims=True)


def start_all(copies):
    for c in copies:
        c.start()


def wait_all(copies):
    for c in copies:
        c.wait()


def coef_a_kernel(meta, s2, s3e, s3o, s5, vec, kh, kl, meh, mel, rh, rl, ch, cl, m_out, y_out, t_out,
                  sbuf, rbh, rbl, cbh, cbl, uh, ul, wh, wl, ssem, usem, wsem, csem):
    even = meta[PAR] == 0
    loads = [pltpu.make_async_copy(s2, sbuf.at[k], ssem.at[k]) for k in range(3)]

    @pl.when(even)
    def _():
        pltpu.make_async_copy(s3e, sbuf.at[1], ssem.at[1]).start()

    @pl.when(jnp.logical_not(even))
    def _():
        pltpu.make_async_copy(s3o, sbuf.at[1], ssem.at[1]).start()

    loads[0].start()
    units = [pltpu.make_async_copy(src.at[k], dst.at[k], usem.at[k, j]) for k in (0, 1) for j, (src, dst) in enumerate(((kh, uh), (kl, ul)))]
    start_all(units)
    wpair = jnp.logical_and(meta[W_PAIR] == 1, meta[W_RIGHT] == 0)
    wcopies = [pltpu.make_async_copy(src.at[0], dst, wsem.at[j]) for j, (src, dst) in enumerate(((meh, wh), (mel, wl)))]
    pl.when(wpair)(lambda: start_all(wcopies))

    @pl.when(meta[W_PAIR] == 1)
    def _():
        pltpu.make_async_copy(s5, sbuf.at[2], ssem.at[2]).start()

    t_out[...] = jnp.zeros_like(t_out)

    def outs(k):
        out = [pltpu.make_async_copy(rbh.at[k], rh.at[k], csem.at[k, 0]), pltpu.make_async_copy(rbl.at[k], rl.at[k], csem.at[k, 1])]
        if k < 2:
            out += [pltpu.make_async_copy(cbh.at[k], ch.at[k], csem.at[k, 2]), pltpu.make_async_copy(cbl.at[k], cl.at[k], csem.at[k, 3])]
        return out

    loads[1].wait()
    left = jnp.where(even, E, X)
    right = jnp.where(even, N, O)
    coef_pair(left, right, False, meta, sbuf.at[1], vec, rbh.at[1], rbl.at[1], cbh.at[1], cbl.at[1], t_out)
    start_all(outs(1))
    loads[0].wait()
    coef_pair(M, N, False, meta, sbuf.at[0], vec, rbh.at[0], rbl.at[0], cbh.at[0], cbl.at[0], t_out)
    start_all(outs(0))
    wait_all(units)
    y_out[0:R, :] = dot3(rbh[1], rbl[1], uh[meta[PAR]], ul[meta[PAR]], NN)
    m_out[0:R, :] = dot3(rbh[0], rbl[0], uh[0], ul[0], NN)

    @pl.when(meta[W_PAIR] == 1)
    def _():
        loads[2].wait()
        w = meta[W_NAME]
        coef_pair(w, w, True, meta, sbuf.at[2], vec, rbh.at[2], rbl.at[2], None, None, t_out)
        start_all(outs(2))

    @pl.when(wpair)
    def _():
        wait_all(wcopies)
        m_out[0:R, :] += dot3(rbh[2], rbl[2], wh[...], wl[...], NN)

    m_out[R : R + 8, 0:R] = t_out[M]
    y_out[R : R + 8, 0:R] = t_out[E]
    pl.when(meta[W_PAIR] == 1)(lambda: wait_all(outs(2)))
    wait_all(outs(0) + outs(1))


def coef_a(meta, scores, vec, k_halves, me_halves):
    half = lambda n: jax.ShapeDtypeStruct((n, R, R), BF16)
    return pl.pallas_call(
        coef_a_kernel,
        out_shape=(half(3), half(3), half(2), half(2), WHOLE, WHOLE, jax.ShapeDtypeStruct((5, 8, R), F32)),
        in_specs=[SMEM_SPEC] + [ANY_SPEC] * 4 + [FULL] + [ANY_SPEC] * 4,
        out_specs=(ANY_SPEC,) * 4 + (FULL,) * 3,
        scratch_shapes=[
            pltpu.VMEM((3, R, R), F32),
            pltpu.VMEM((3, R, R), BF16),
            pltpu.VMEM((3, R, R), BF16),
            pltpu.VMEM((2, R, R), BF16),
            pltpu.VMEM((2, R, R), BF16),
            pltpu.VMEM((2, R, F), BF16),
            pltpu.VMEM((2, R, F), BF16),
            pltpu.VMEM((R, F), BF16),
            pltpu.VMEM((R, F), BF16),
            pltpu.SemaphoreType.DMA((3,)),
            pltpu.SemaphoreType.DMA((2, 2)),
            pltpu.SemaphoreType.DMA((2,)),
            pltpu.SemaphoreType.DMA((3, 4)),
        ],
        compiler_params=PARAMS,
        cost_estimate=COST,
        name="coef_a",
    )(meta, *scores, vec, *k_halves, *me_halves)


def coef_b_kernel(meta, s0, s1, vec, nh, nl, ta, rh, rl, ch, cl, t_out, x_out):
    k = pl.program_id(0)

    @pl.when(k == 0)
    def _():
        t_out[...] = jnp.zeros_like(t_out)
        coef_pair(O, N, False, meta, s0, vec, rh.at[0], rl.at[0], ch.at[0], cl.at[0], t_out)

    @pl.when(k == 1)
    def _():
        coef_pair(X, N, False, meta, s1, vec, rh.at[0], rl.at[0], ch.at[0], cl.at[0], t_out)
        x_out[0:R, :] = dot3(rh[0], rl[0], nh[0], nl[0], NN)
        x_out[R : R + 8, 0:R] = ta[X] + t_out[X]


def coef_b(meta, s0, s1, vec, units, ta):
    half = jax.ShapeDtypeStruct((2, R, R), BF16)
    one = pl.BlockSpec((1, R, R), lambda k: (k, 0, 0))
    mat = pl.BlockSpec((R, R), lambda k: (0, 0))
    stay = pl.BlockSpec((5, 8, R), lambda k: (0, 0, 0))
    unit = pl.BlockSpec((1, R, F), lambda k: (0, 0, 0))
    return pl.pallas_call(
        coef_b_kernel,
        grid=(2,),
        out_shape=(half,) * 4 + (jax.ShapeDtypeStruct((5, 8, R), F32), WHOLE),
        in_specs=[SMEM_SPEC, mat, mat, stay, unit, unit, stay],
        out_specs=(one,) * 4 + (stay, pl.BlockSpec((R + 8, F), lambda k: (0, 0))),
        compiler_params=PARAMS,
        cost_estimate=COST,
        name="coef_b",
    )(meta, s0, s1, vec, *units, ta)


def right_kernel(part, meta, chb, clb, cha, cla, rha, rla, kh, kl, meh, mel, ta, tb, *refs):
    if part == 0:
        m, swap, out, left, cbh, cbl, ubh, ubl, mbuf, wbuf, sem, msem = refs
        mcopies = [pltpu.make_async_copy(src, dst, msem.at[k]) for k, (src, dst) in enumerate(((m, mbuf), (swap, wbuf)))]
        l_copy = pltpu.make_async_copy(mbuf, left, msem.at[2])
    else:
        out, cbh, cbl, ubh, ubl, sem = refs
    at = pl.ds(part * (F // 2), F // 2)
    terms = (
        (chb.at[0], clb.at[0], kh.at[1, :, at], kl.at[1, :, at]),
        (chb.at[1], clb.at[1], kh.at[2, :, at], kl.at[2, :, at]),
        (cha.at[0], cla.at[0], meh.at[0, :, at], mel.at[0, :, at]),
        (cha.at[1], cla.at[1], meh.at[1, :, at], mel.at[1, :, at]),
        (rha.at[2], rla.at[2], kh.at[0, :, at], kl.at[0, :, at]),
    )

    def copies(t):
        return [pltpu.make_async_copy(src, dst.at[t], sem.at[t, j]) for j, (src, dst) in enumerate(zip(terms[t], (cbh, cbl, ubh, ubl)))]

    def term(t):
        wait_all(copies(t))
        v = dot3(cbh[t], cbl[t], ubh[t], ubl[t], NN if t == 4 else TN)
        if t == 0:
            out[0:R, :] = v
        else:
            out[0:R, :] += v

    even = meta[EVEN] == 1
    wright = jnp.logical_and(meta[W_PAIR] == 1, meta[W_RIGHT] == 1)
    for t in range(3):
        start_all(copies(t))
    pl.when(even)(lambda: start_all(copies(3)))
    pl.when(wright)(lambda: start_all(copies(4)))
    if part == 0:
        start_all(mcopies)
        out[R : R + 8, 0:R] = ta[N] + tb[N]
    term(0)
    if part == 0:
        wait_all(mcopies)

        @pl.when(jnp.logical_not(even))
        def _():
            mbuf[...] += wbuf[...]

        l_copy.start()
    term(1)
    term(2)
    pl.when(even)(lambda: term(3))
    pl.when(wright)(lambda: term(4))
    if part == 0:
        l_copy.wait()


def right_part(part, meta, mats, units, ta, tb, more=()):
    thin = jax.ShapeDtypeStruct((R + 8 * (1 - part), F // 2), F32)
    return pl.pallas_call(
        functools.partial(right_kernel, part),
        out_shape=thin if part else (thin, WHOLE),
        in_specs=[SMEM_SPEC] + [ANY_SPEC] * 10 + [FULL] * 2 + [ANY_SPEC] * len(more),
        out_specs=FULL if part else (FULL, ANY_SPEC),
        scratch_shapes=[
            pltpu.VMEM((5, R, R), BF16),
            pltpu.VMEM((5, R, R), BF16),
            pltpu.VMEM((5, R, F // 2), BF16),
            pltpu.VMEM((5, R, F // 2), BF16),
        ]
        + [pltpu.VMEM((R + 8, F), F32)] * len(more)
        + [pltpu.SemaphoreType.DMA((5, 4))]
        + [pltpu.SemaphoreType.DMA((3,))] * (len(more) // 2),
        compiler_params=pltpu.CompilerParams(vmem_limit_bytes=48 * 1024 * 1024),
        cost_estimate=COST,
        name="right_part",
    )(meta, *mats, *units, ta, tb, *more)


def own_kernel(meta, s4, rhb, rlb, cha, cla, kh, kl, vec, ta, tb, more, swap, out, sbuf, cbh, cbl, ubh, ubl, t, mbuf, ssem, csem, usem, msem):
    odd = meta[ODD] == 1
    pair = meta[OWN_PAIR] == 1
    load = pltpu.make_async_copy(s4, sbuf, ssem)
    pl.when(pair)(load.start)
    units = [pltpu.make_async_copy(src.at[k], dst.at[k], usem.at[k, j]) for k in range(3) for j, (src, dst) in enumerate(((kh, ubh), (kl, ubl)))]
    mats = [pltpu.make_async_copy(src.at[0], dst.at[0], csem.at[0, j]) for j, (src, dst) in enumerate(((rhb, cbh), (rlb, cbl)))]
    mats += [pltpu.make_async_copy(src.at[1], dst.at[1], csem.at[1, j]) for j, (src, dst) in enumerate(((cha, cbh), (cla, cbl)))]
    start_all(units + mats)
    adds = [pltpu.make_async_copy(src, mbuf.at[j], msem.at[j]) for j, src in enumerate((more, swap))]
    start_all(adds)
    t[...] = ta[...] + tb[...]
    wait_all(units + mats)
    out[0:R, :] = dot3(cbh[0], cbl[0], ubh[0], ubl[0], NN)

    @pl.when(odd)
    def _():
        out[0:R, :] += dot3(cbh[1], cbl[1], ubh[2], ubl[2], TN)

    @pl.when(pair)
    def _():
        load.wait()
        coef_pair(O, O, True, meta, sbuf, vec, cbh.at[2], cbl.at[2], None, None, t)
        out[0:R, :] += dot3(cbh[2], cbl[2], ubh[1], ubl[1], NN)

    out[R : R + 8, 0:R] = t[O]
    wait_all(adds)
    out[...] += mbuf[0]

    @pl.when(jnp.logical_not(odd))
    def _():
        out[...] += mbuf[1]


def own_part(meta, s4, rows, cols, units, vec, ta, tb, more, swap):
    return pl.pallas_call(
        own_kernel,
        out_shape=WHOLE,
        in_specs=[SMEM_SPEC] + [ANY_SPEC] * 7 + [FULL] * 3 + [ANY_SPEC] * 2,
        out_specs=FULL,
        scratch_shapes=[
            pltpu.VMEM((R, R), F32),
            pltpu.VMEM((3, R, R), BF16),
            pltpu.VMEM((3, R, R), BF16),
            pltpu.VMEM((3, R, F), BF16),
            pltpu.VMEM((3, R, F), BF16),
            pltpu.VMEM((5, 8, R), F32),
            pltpu.VMEM((2, R + 8, F), F32),
            pltpu.SemaphoreType.DMA,
            pltpu.SemaphoreType.DMA((2, 2)),
            pltpu.SemaphoreType.DMA((3, 2)),
            pltpu.SemaphoreType.DMA((2,)),
        ],
        compiler_params=pltpu.CompilerParams(vmem_limit_bytes=48 * 1024 * 1024),
        cost_estimate=COST,
        name="own_part",
    )(meta, s4, *rows, *cols, *units, vec, ta, tb, more, swap)


def grads_kernel(right, left, left2, own, kept, vec, out, rb, lb, l2b, ob, kb, gb, sem, tsem):
    T = 128
    chunks = [slice(k * T, (k + 1) * T) for k in range(R // T)]
    srcs = ((right, rb), (left, lb), (left2, l2b), (own, ob), (kept, kb))
    tails = [pltpu.make_async_copy(src.at[R : R + 8], dst.at[R : R + 8], tsem.at[k]) for k, (src, dst) in enumerate(((right, rb), (left, lb), (kept, kb)))]
    start_all(tails)
    loads = [[pltpu.make_async_copy(src.at[at], dst.at[at], sem.at[k, j]) for j, (src, dst) in enumerate(srcs)] for k, at in enumerate(chunks)]
    stores = [pltpu.make_async_copy(gb.at[at], out.at[at], sem.at[k, 5]) for k, at in enumerate(chunks)]
    for load in loads:
        start_all(load)
    wait_all(tails)
    along = jnp.transpose(rb[R : R + 8, 0:R] + lb[R : R + 8, 0:R] + kb[R : R + 8, 0:R])[:, 0:1]
    inv = jnp.transpose(vec[O])[:, 0:1]
    scale = inv * along
    for k, at in enumerate(chunks):
        wait_all(loads[k])
        for part, cols in ((lb, slice(0, F // 2)), (l2b, slice(F // 2, F))):
            grad = kb[at, cols] + rb[at, cols] + part[at, :]
            gb[at, cols] = (grad * 10.0 - ob[at, cols] * scale[at]) * inv[at]
        stores[k].start()
    wait_all(stores)


def grads_of(kept, right, left, left2, own, vec):
    return pl.pallas_call(
        grads_kernel,
        out_shape=jax.ShapeDtypeStruct((R, F), F32),
        in_specs=[ANY_SPEC] * 5 + [FULL],
        out_specs=ANY_SPEC,
        scratch_shapes=[
            pltpu.VMEM((R + 8, F), F32),
            pltpu.VMEM((R + 8, F // 2), F32),
            pltpu.VMEM((R, F // 2), F32),
            pltpu.VMEM((R, F), F32),
            pltpu.VMEM((R + 8, F), F32),
            pltpu.VMEM((R, F), F32),
            pltpu.SemaphoreType.DMA((4, 6)),
            pltpu.SemaphoreType.DMA((3,)),
        ],
        compiler_params=pltpu.CompilerParams(vmem_limit_bytes=20 * 1024 * 1024),
        name="grads",
    )(right, left, left2, own, kept, vec)


def per_device(embeddings, partner):
    blk = lax.axis_index("blk")
    count = lax.axis_size("blk")
    par = (blk % 2).astype(jnp.int32)
    even = par == 0
    row = (blk // 2) % 4
    inner = jnp.logical_or(row == 1, row == 2)

    def is_inner(i):
        return (i // 2) % 4 in (1, 2)

    def shift(v, steps):
        return lax.ppermute(v, "blk", [(i, (i + steps) % count) for i in range(count)])

    def cores(v):
        return lax.ppermute(v, "blk", [(i, i ^ 1) for i in range(count)])

    def outwards(v):
        return lax.ppermute(v, "blk", [(i, (i + (2 if i % 2 else -2)) % count) for i in range(count)])

    def feats(v, where=None):
        if where is None:
            return lax.ppermute(v, "feat", [(0, 1), (1, 0)])
        pairs = [(2 * i + f, 2 * i + 1 - f) for i in range(count) if where(i) for f in (0, 1)]
        return lax.ppermute(v, ("blk", "feat"), pairs)

    own = embeddings
    line = jnp.pad(partner.astype(F32)[None], ((0, 7), (0, F - R)))
    block = jnp.concatenate([own, line], axis=0)
    right = shift(block, -2)
    left = shift(block, 2)
    other = cores(block)
    names = jnp.stack([blk + count - 2, blk + count - 1, blk, blk + 1 - 2 * par, blk + 2]) % count
    own_pair = jnp.logical_or(inner, par == 1).astype(jnp.int32)
    w_pair = jnp.logical_and(inner, par == 0).astype(jnp.int32)
    w_right = (row == 2).astype(jnp.int32)
    flags = jnp.stack([own_pair, w_pair, w_right * N, w_right, 1 - par, par, jnp.ones_like(par)])
    meta = jnp.concatenate([par[None], names.astype(jnp.int32) * R, flags.astype(jnp.int32)])

    s_rows = lambda n: jax.ShapeDtypeStruct((n * R + 8, R), F32)
    own_pairs = lambda i: i % 2 == 1 or is_inner(i)
    w_pairs = lambda i: i % 2 == 0 and is_inner(i)
    p4, p3o = scores_call(near_kernel, "near_scores", (meta, block, other), (s_rows(1), s_rows(1)), 2, 2, True)
    g4, g3o = feats(p4, own_pairs), feats(p3o, lambda i: i % 2 == 1)
    extra = lax.ppermute(left, "blk", [(i + 1, i) for i in range(0, count, 2)])
    right, g4, g3o = lax.optimization_barrier((right, g4, g3o))
    far, kh, kl = scores_call(
        far_a_kernel, "far_scores_a", (meta, block, other, right), (s_rows(2), halves(3), halves(3)), 3, 2, True
    )
    far_g = feats(far)
    left, extra, kh = lax.optimization_barrier((left, extra, kh))
    p2, p3e, p5, meh, mel = scores_call(
        far_b_kernel, "far_scores_b", (meta, left, extra, right), (s_rows(1), MAT, MAT, halves(2), halves(2)), 3, 3, True
    )
    g2, g3e, g5 = feats(p2), feats(p3e, lambda i: i % 2 == 0), feats(p5, w_pairs)

    def inverse(mine, theirs):
        return 1.0 / jnp.sqrt(mine + theirs + 1e-06)

    def vectors(cells):
        zero = jnp.zeros((R,), F32)
        return jnp.stack([jnp.stack(c + [zero] * (8 - len(c))) for c in cells])

    who = lambda b: b[R, 0:R]
    inv_nox = inverse(far[2 * R : 2 * R + 3], far_g[2 * R : 2 * R + 3])
    inv_me = inverse(p2[R : R + 2], g2[R : R + 2])
    packs = [
        [inv_me[0], who(left)],
        [inv_me[1], who(extra)],
        [inv_nox[1], who(block)],
        [inv_nox[2], who(other)],
        [inv_nox[0], who(right)],
    ]
    vec_a = vectors([[], []] + packs[2:])
    near_inv = jnp.where(even, inverse(p4[R : R + 2], g4[R : R + 2]), inverse(p3o[R : R + 2], g3o[R : R + 2]))
    vec_near = vectors([[], [], [near_inv[0], who(block)], [near_inv[1], who(other)], []])
    sums = []

    def pair(*args, **kw):
        s, t, p = pair_sums(meta, *args, **kw)
        sums.append((t[:, 0:2], p))
        return s

    s4 = pair(p4, g4, vec_near, O, O, active=OWN_PAIR)
    s3o = pair(p3o, g3o, vec_near, X, O, active=ODD)
    s0 = pair(far, far_g, vec_a, O, N)
    s1 = pair(far, far_g, vec_a, X, N, first=2)
    vec_b = vectors(packs)
    s3e = pair(p3e, g3e, vec_b, E, N, active=EVEN)
    s5 = pair(p5, g5, vec_b, None, None, active=W_PAIR)
    s2 = pair(p2, g2, vec_b, M, N)

    t = sum(v for v, _ in sums)
    p = jnp.sum(sum(v for _, v in sums), axis=0)
    zero = jnp.zeros((2, R), F32)
    spos = jnp.stack([p, p * 0.0])
    chip = jnp.where(
        even, jnp.stack([t[M], t[E], t[O], t[X], t[N], zero, spos]), jnp.stack([zero, t[M], t[X], t[O], zero, t[N], spos])
    )
    chip = chip + cores(chip)
    got = outwards(jnp.where(even, chip[0:2], chip[4:6]))
    total = chip[2:4] + (got + cores(got))
    counts = total[:, 1] + 1.0
    a = counts * 0.5 / total[:, 0]
    loss = jnp.sum(counts * (10.0 + jnp.log(total[:, 0]))) * 0.5 - jnp.sum(chip[6, 0])
    a_one = outwards(jnp.concatenate([a, jnp.full((1, R), loss, F32)], axis=0))
    a_two = cores(a_one)
    a_l, a_r = jnp.where(even, a_two, a_one), jnp.where(even, a_one, a_two)
    mine = lambda v: jnp.where(even, v[0], v[1])
    a_all = [mine(a_l), a_l[1], mine(a), mine(a[::-1]), mine(a_r)]
    vec = vectors([p + [q] for p, q in zip(packs, a_all)])
    loss = loss + jnp.where(row % 2 == 0, a_r[2, 0], a_l[2, 0])

    def both(v, k):
        return v + lax.ppermute(v, "blk", [(i, i ^ k) for i in range(count)])

    rha, rla, cha, cla, to_left, swap, ta = coef_a(meta, (s2, s3e, s3o, s5), vec, (kh, kl), (meh, mel))
    swapped = cores(swap)
    vec, ta = lax.optimization_barrier((vec, ta))
    rhb, rlb, chb, clb, tb, to_other = coef_b(meta, s0, s1, vec, (kh, kl), ta)
    loss = both(loss, 4)
    tb, loss = lax.optimization_barrier((tb, loss))
    mats, units = (chb, clb, cha, cla, rha, rla), (kh, kl, meh, mel)
    to_right, to_left = right_part(0, meta, mats, units, ta, tb, (to_left, swapped))
    from_right = shift(to_left, -2)
    from_left = shift(to_right, 2)
    clb, to_right = lax.optimization_barrier((clb, to_right))
    mats = (chb, clb, cha, cla, rha, rla)
    to_right_2 = right_part(1, meta, mats, units, ta, tb)
    from_left_2 = shift(to_right_2, 2)
    loss, to_right_2 = lax.optimization_barrier((loss, to_right_2))
    from_other = cores(to_other)
    loss = both(both(loss, 16), 32)
    loss, rhb = lax.optimization_barrier((loss, rhb))
    kept = own_part(meta, s4, (rhb, rlb), (cha, cla), (kh, kl), vec, ta, tb, from_other, swapped)
    loss, kept = lax.optimization_barrier((loss, kept))
    loss = both(loss, 8) / (count * R)
    grads = grads_of(kept, from_right, from_left, from_left_2, own, vec)
    grads, loss = lax.optimization_barrier((grads, loss))
    return (loss, grads)


def solution(mesh):
    in_specs = (P("blk", "feat"), P("blk"))
    out_specs = (P(), P("blk", "feat"))
    return jax.shard_map(per_device, mesh=mesh, in_specs=in_specs, out_specs=out_specs, check_vma=False)
```
